32 devices in a mesh: sample: 2 (over core), prefix: 16 (over z, y, x).
Axes of the slice: x: 2, y: 2, z: 4, core: 2. Of those that a mesh axis runs over, the one named last changes fastest.
Arguments:
- resp_q: bfloat16 [32, 128, 4096], P(('sample', 'prefix')), may hold values from -6 to 6
- resp_k: bfloat16 [32, 128, 512], P(('sample', 'prefix')), may hold values from -6 to 6
- resp_v: bfloat16 [32, 128, 512], P(('sample', 'prefix')), may hold values from -6 to 6
- resp_do: bfloat16 [32, 128, 4096], P(('sample', 'prefix')), may hold values from -6 to 6
- resp_out: bfloat16 [32, 128, 4096], P(('sample', 'prefix')), may hold values from -6 to 6
- resp_lse: float32 [32, 128, 32], P(('sample', 'prefix'))
- prompt_k: bfloat16 [256, 512], P('prefix'), may hold values from -6 to 6
- prompt_v: bfloat16 [256, 512], P('prefix'), may hold values from -6 to 6
- resp_lengths: int32 [32], P(('sample', 'prefix')), may hold values from 16 to 128, as said below
Outputs:
- resp_dq: bfloat16 [32, 128, 4096], P(('sample', 'prefix'))
- resp_dk: bfloat16 [32, 128, 512], P(('sample', 'prefix'))
- resp_dv: bfloat16 [32, 128, 512], P(('sample', 'prefix'))
- prompt_dk: float32 [256, 512], P('prefix')
- prompt_dv: float32 [256, 512], P('prefix')
The draws below stay inside these ranges and needn't reach their ends.
Inputs may be any that keep to these rules, and one draw needn't show every extreme that they name: `resp_lengths`: some response has exactly 128 live tokens and some has 16.
All inputs are finite; a program needn't handle non-finite values.
Results may differ from the reference program's by a relative error of at most 0.0051.
Values may be sent and summed in bfloat16 or wider, within the bound.
A program may use at most 64 MiB of HBM per device.

```python
import jax
import jax.numpy as jnp
from jax import lax

H = 32
KVH = 4
HD = 128
R = 128
RESP = 32
P_SIZE = 256


def draw_resp_lse(key, part):
    key = jax.random.fold_in(key, 11)
    positions = jnp.arange(R, dtype=jnp.float32)
    baseline = jnp.log(P_SIZE + positions + 1.0)[None, :, None]
    offset = 0.5 + jnp.clip(0.25 * jax.random.normal(key, (RESP, R, H), jnp.float32), -0.5, 0.5)
    return baseline + offset


def draw_resp_lengths(key, part):
    key = jax.random.fold_in(key, 23)
    first_key, second_key = jax.random.split(key)
    picked = jax.random.randint(first_key, (RESP,), R // 8, R + 1)
    order = jax.random.permutation(second_key, RESP)
    picked = picked.at[order[0]].set(R)
    picked = picked.at[order[1]].set(R // 8)
    return picked.astype(jnp.int32)


def steps_of(key, shape, pieces, low, top_value):
    level = 1.0
    for position, blocks in pieces:
        draws = jax.random.uniform(jax.random.fold_in(jax.random.fold_in(key, 6), position), (blocks,), jnp.float32, low / len(pieces), top_value / len(pieces))
        level = level * jnp.repeat(jnp.exp(draws), shape[position] // blocks).reshape((-1,) + (1,) * (len(shape) - 1 - position))
    return level


def scatter_about(stream_key, dims, deviation, bound, cuts=(), kind=jnp.bfloat16):
    gain = steps_of(stream_key, dims, cuts, -0.22, 0.18) if cuts else 1.0
    values = jax.random.normal(stream_key, dims, jnp.float32) * deviation * gain
    return jnp.minimum(jnp.maximum(values, -bound), bound).astype(kind)


def setup_inputs(seed: int = 0) -> dict:
    splits = jax.random.split(jax.random.key(seed), 10)
    resp_q = scatter_about(splits[0], (RESP, R, H * HD), 1.0, 6.0, ((0, 32),))
    resp_k = scatter_about(splits[1], (RESP, R, KVH * HD), 1.0, 6.0, ((0, 32),))
    resp_v = scatter_about(splits[2], (RESP, R, KVH * HD), 1.0, 6.0, ((0, 32),))
    resp_do = scatter_about(splits[3], (RESP, R, H * HD), 1.0, 6.0, ((0, 32),))
    resp_out = scatter_about(splits[4], (RESP, R, H * HD), 1.0, 6.0, ((0, 32),))
    resp_lse = draw_resp_lse(jax.random.fold_in(splits[9], 71), 0)
    prompt_k = scatter_about(splits[6], (P_SIZE, KVH * HD), 1.0, 6.0, ((0, 16),))
    prompt_v = scatter_about(splits[7], (P_SIZE, KVH * HD), 1.0, 6.0, ((0, 16),))
    resp_lengths = draw_resp_lengths(jax.random.fold_in(splits[9], 71), 0)
    return {"resp_q": resp_q, "resp_k": resp_k, "resp_v": resp_v, "resp_do": resp_do, "resp_out": resp_out, "resp_lse": resp_lse, "prompt_k": prompt_k, "prompt_v": prompt_v, "resp_lengths": resp_lengths}


def reference(resp_q, resp_k, resp_v, resp_do, resp_out, resp_lse, prompt_k, prompt_v, resp_lengths):
    groups = H // KVH
    score_scale = HD ** -0.5
    key_count = P_SIZE + R
    query_pos = jnp.arange(R, dtype=jnp.int32)
    key_pos = jnp.arange(key_count, dtype=jnp.int32)

    def one_response(response_items):
        queries, own_keys, own_values, grad_out, fwd_out, lse_rows, length = response_items
        all_keys = jnp.concatenate([prompt_k, own_keys], 0).astype(jnp.float32).reshape(key_count, KVH, HD).transpose(1, 0, 2)
        all_values = jnp.concatenate([prompt_v, own_values], 0).astype(jnp.float32).reshape(key_count, KVH, HD).transpose(1, 0, 2)
        live = (query_pos[:, None] < length) & ((key_pos[None, :] < P_SIZE) | (key_pos[None, :] - P_SIZE <= query_pos[:, None]))
        live_mask = live.astype(jnp.float32)
        query_heads = queries.astype(jnp.float32).reshape(R, KVH, groups, HD).transpose(1, 0, 2, 3)
        grad_heads = grad_out.astype(jnp.float32).reshape(R, KVH, groups, HD).transpose(1, 0, 2, 3)
        out_heads = fwd_out.astype(jnp.float32).reshape(R, KVH, groups, HD).transpose(1, 0, 2, 3)
        out_dot = jnp.sum(grad_heads * out_heads, -1)
        lse_heads = lse_rows.reshape(R, KVH, groups).transpose(1, 0, 2)

        def per_group(group_items):
            query_x, grad_x, key_x, value_x, dot_x, lse_x = group_items
            scores = jnp.einsum('tgd,ud->gtu', query_x, key_x) * score_scale
            probs = jnp.exp(scores - lse_x.T[:, :, None]) * live_mask[None]
            prob_grad = jnp.einsum('tgd,ud->gtu', grad_x, value_x)
            score_grad = probs * (prob_grad - dot_x.T[:, :, None])
            probs_low = lax.optimization_barrier(probs.astype(jnp.bfloat16)).astype(jnp.float32)
            score_low = lax.optimization_barrier(score_grad.astype(jnp.bfloat16)).astype(jnp.float32)
            query_grad = jnp.einsum('gtu,ud->tgd', score_low, key_x) * score_scale
            key_grad = jnp.einsum('gtu,tgd->ud', score_low, query_x) * score_scale
            value_grad = jnp.einsum('gtu,tgd->ud', probs_low, grad_x)
            return query_grad, key_grad, value_grad

        query_grad, key_grad, value_grad = lax.map(per_group, (query_heads, grad_heads, all_keys, all_values, out_dot, lse_heads))
        query_grad = query_grad.transpose(1, 0, 2, 3).reshape(R, H * HD).astype(jnp.bfloat16)
        key_grad = key_grad.transpose(1, 0, 2).reshape(key_count, KVH * HD)
        value_grad = value_grad.transpose(1, 0, 2).reshape(key_count, KVH * HD)
        return query_grad, key_grad[P_SIZE:].astype(jnp.bfloat16), value_grad[P_SIZE:].astype(jnp.bfloat16), key_grad[:P_SIZE], value_grad[:P_SIZE]

    def accumulate(carry, response_items):
        outputs = one_response(response_items)
        return (carry[0] + outputs[3], carry[1] + outputs[4]), (outputs[0], outputs[1], outputs[2])

    start = (jnp.zeros((P_SIZE, KVH * HD), jnp.float32), jnp.zeros((P_SIZE, KVH * HD), jnp.float32))
    sums, per_resp = lax.scan(accumulate, start, (resp_q, resp_k, resp_v, resp_do, resp_out, resp_lse, resp_lengths))
    return per_resp[0], per_resp[1], per_resp[2], sums[0], sums[1]
```

```python
import functools
import math

import jax
import jax.numpy as jnp
from jax import lax
from jax.experimental import pallas as pl
from jax.experimental.pallas import tpu as pltpu
from jax.sharding import PartitionSpec as P

H = 32
KVH = 4
HD = 128
G = H // KVH
MESH = pl.DeviceIdType.MESH
NT = (((1,), (1,)), ((), ()))
LOG2E = math.log2(math.e)
SCALE = HD ** (-0.5)
UB = 256


def dot(a, b):
    return jnp.dot(a, b, preferred_element_type=jnp.float32)


def dot_nt(a, b):
    return lax.dot_general(a, b, NT, preferred_element_type=jnp.float32)


def heads_to_rows(block):
    return jnp.concatenate([block[:, g * HD : (g + 1) * HD] for g in range(G)], 0)


def rows_to_lanes(block):
    return jnp.concatenate([block[g : g + 1] for g in range(G)], 1)


def part_grads(keys, values, queries, grads, lse_row, delta_row, live):
    scores = dot_nt(keys, queries)
    probs = jnp.exp2(scores * (SCALE * LOG2E) - lse_row)
    if live is not None:
        probs = jnp.where(live, probs, 0.0)
    prob_grad = dot_nt(values, grads)
    score_low = (probs * (prob_grad - delta_row)).astype(jnp.bfloat16)
    probs_low = probs.astype(jnp.bfloat16)
    dq_t = dot(keys.T, score_low)
    dk = dot(score_low, queries) * SCALE
    dv = dot(probs_low, grads)
    return dq_t, dk, dv


def kernel(
    n, ns, rows, length_ref, q_hbm, k_hbm, v_hbm, do_hbm, out_hbm, lse_hbm, pk_hbm, pv_hbm,
    dq_hbm, dk_ref, dv_ref, pdk_ref, pdv_ref,
    q_ref, k_ref, v_ref, do_ref, out_ref, lse_ref, pk_ref, pv_ref, dq_ref, lse_t, delta_t, dq_acc,
    gathered, parts, landed, totals,
    load_sem, store_sem, gather_send, gather_recv, part_send, part_recv, total_send, total_recv,
):
    tokens = q_ref.shape[0]
    me = lax.axis_index("prefix")
    mine = lax.axis_index("sample")

    pairs = [
        (pk_hbm, pk_ref), (pv_hbm, pv_ref), (do_hbm.at[0], do_ref), (out_hbm.at[0], out_ref),
        (lse_hbm.at[0], lse_ref), (q_hbm.at[0], q_ref), (k_hbm.at[0], k_ref), (v_hbm.at[0], v_ref),
    ]
    loads = [pltpu.make_async_copy(a, b, load_sem.at[i]) for i, (a, b) in enumerate(pairs)]
    for copy in loads:
        copy.start()

    barrier = pltpu.get_barrier_semaphore()

    def greet(d, _):
        pl.semaphore_signal(
            barrier, inc=1, device_id={"prefix": lax.rem(me + d, n)}, device_id_type=MESH
        )
        return 0

    def greet_sample(d, _):
        pl.semaphore_signal(
            barrier, inc=1, device_id={"sample": lax.rem(mine + d, ns)}, device_id_type=MESH
        )
        return 0

    lax.fori_loop(1, n, greet, 0)
    lax.fori_loop(1, ns, greet_sample, 0)
    loads[0].wait()
    loads[1].wait()
    width = KVH * HD
    gathered[0:rows, :width] = pk_ref[...]
    gathered[0:rows, width:] = pv_ref[...]
    pl.semaphore_wait(barrier, n - 1 + ns - 1)

    def gather_copy(d):
        return pltpu.make_async_remote_copy(
            src_ref=gathered.at[pl.ds(0, rows)],
            dst_ref=gathered.at[pl.ds(pl.multiple_of(d * rows, rows), rows)],
            send_sem=gather_send.at[d],
            recv_sem=gather_recv.at[d],
            device_id={"prefix": lax.rem(me + d, n)},
            device_id_type=MESH,
        )

    def start_gather(d, _):
        gather_copy(d).start()
        return 0

    lax.fori_loop(1, n, start_gather, 0)

    for copy in loads[2:]:
        copy.wait()
    length = length_ref[0]
    key_pos = lax.broadcasted_iota(jnp.int32, (tokens, tokens), 0)
    query_pos = lax.broadcasted_iota(jnp.int32, (tokens, tokens), 1)
    causal = key_pos <= query_pos
    live_t = lax.broadcasted_iota(jnp.int32, (H, tokens), 1) < length
    lse_t[...] = jnp.where(live_t, lse_ref[...].T * LOG2E, 1e30)

    def own_step(j, _):
        cols = pl.ds(pl.multiple_of(j * G * HD, G * HD), G * HD)
        head = pl.ds(pl.multiple_of(j * HD, HD), HD)
        stat = pl.ds(pl.multiple_of(j * G, G), G)
        queries = heads_to_rows(q_ref[:, cols])
        grads = heads_to_rows(do_ref[:, cols])
        outs = heads_to_rows(out_ref[:, cols])
        product = grads.astype(jnp.float32) * outs.astype(jnp.float32)
        high = product.astype(jnp.bfloat16)
        low = (product - high.astype(jnp.float32)).astype(jnp.bfloat16)
        ones = jnp.ones((G, HD), jnp.bfloat16)
        sums = dot_nt(ones, high) + dot_nt(ones, low)
        delta_row = sums[0:1]
        for g in range(G):
            delta_t[j, g : g + 1, :] = delta_row[:, g * HD : (g + 1) * HD]
        lse_row = rows_to_lanes(lse_t[stat, :])
        live = jnp.concatenate([causal] * G, 1)
        dq_t, dk, dv = part_grads(
            k_ref[:, head], v_ref[:, head], queries, grads, lse_row, delta_row, live
        )
        dq_acc[j] = dq_t
        dk_ref[0, :, head] = dk.astype(jnp.bfloat16)
        dv_ref[0, :, head] = dv.astype(jnp.bfloat16)
        return 0

    lax.fori_loop(0, KVH, own_step, 0)

    def wait_gather(d, _):
        gather_copy(d).wait()
        return 0

    lax.fori_loop(1, n, wait_gather, 0)

    def part_copy(j, d):
        return pltpu.make_async_remote_copy(
            src_ref=parts.at[j, d],
            dst_ref=landed.at[j, d],
            send_sem=part_send.at[j, d],
            recv_sem=part_recv.at[j, d],
            device_id={"prefix": lax.rem(me + n - d, n)},
            device_id_type=MESH,
        )

    prompt_rows = n * rows
    block = UB if prompt_rows % UB == 0 else prompt_rows

    def prompt_step(j, _):
        cols = pl.ds(pl.multiple_of(j * G * HD, G * HD), G * HD)
        head = pl.ds(pl.multiple_of(j * HD, HD), HD)
        head_v = pl.ds(pl.multiple_of(j * HD + width, HD), HD)
        stat = pl.ds(pl.multiple_of(j * G, G), G)
        queries = heads_to_rows(q_ref[:, cols])
        grads = heads_to_rows(do_ref[:, cols])
        lse_row = rows_to_lanes(lse_t[stat, :])
        delta_row = rows_to_lanes(delta_t[j])

        def block_step(b, _):
            at = pl.ds(pl.multiple_of(b * block, block), block)
            dq_t, dk, dv = part_grads(
                gathered[at, head], gathered[at, head_v], queries, grads, lse_row, delta_row, None
            )
            dq_acc[j] += dq_t
            both = jnp.concatenate([dk, dv], 1).astype(jnp.bfloat16)
            slots = pl.ds(b * (block // rows), block // rows)
            parts[j, slots] = both.reshape(block // rows, rows, 2 * HD)
            return 0

        if prompt_rows == block:
            block_step(0, 0)
        else:
            lax.fori_loop(0, prompt_rows // block, block_step, 0)

        def start_part(d, _):
            part_copy(j, d).start()
            return 0

        lax.fori_loop(1, n, start_part, 0)
        landed[j, 0] = parts[j, 0]
        dq_t = (dq_acc[j] * SCALE).astype(jnp.bfloat16)
        for g in range(G):
            at = pl.ds(pl.multiple_of((j * G + g) * HD, HD), HD)
            dq_ref[:, at] = dq_t[:, g * HD : (g + 1) * HD].T
        return 0

    lax.fori_loop(0, KVH, prompt_step, 0)
    store = pltpu.make_async_copy(dq_ref, dq_hbm.at[0], store_sem)
    store.start()

    def sum_step(j, _):
        def wait_part(d, _):
            part_copy(j, d).wait()
            return 0

        lax.fori_loop(1, n, wait_part, 0)
        totals[mine, j] = jnp.sum(landed[j].astype(jnp.float32), 0)
        return 0

    lax.fori_loop(0, KVH, sum_step, 0)

    def total_copy(d):
        return pltpu.make_async_remote_copy(
            src_ref=totals.at[mine],
            dst_ref=totals.at[mine],
            send_sem=total_send.at[d],
            recv_sem=total_recv.at[d],
            device_id={"sample": lax.rem(mine + d, ns)},
            device_id_type=MESH,
        )

    for d in range(1, ns):
        total_copy(d).start()
    for d in range(1, ns):
        total_copy(d).wait()
    for j in range(KVH):
        both = totals[0, j]
        for s in range(1, ns):
            both = both + totals[s, j]
        pdk_ref[:, j * HD : (j + 1) * HD] = both[:, :HD]
        pdv_ref[:, j * HD : (j + 1) * HD] = both[:, HD:]
    store.wait()


def body(resp_q, resp_k, resp_v, resp_do, resp_out, resp_lse, prompt_k, prompt_v, resp_lengths):
    n = lax.axis_size("prefix")
    ns = lax.axis_size("sample")
    rows, width = prompt_k.shape
    _, tokens, q_width = resp_q.shape
    bf16, f32 = jnp.bfloat16, jnp.float32
    vmem = pl.BlockSpec(memory_space=pltpu.VMEM)
    hbm = pl.BlockSpec(memory_space=pl.ANY)
    dma = pltpu.SemaphoreType.DMA
    return pl.pallas_call(
        functools.partial(kernel, n, ns, rows),
        out_shape=(
            jax.ShapeDtypeStruct(resp_q.shape, bf16),
            jax.ShapeDtypeStruct(resp_k.shape, bf16),
            jax.ShapeDtypeStruct(resp_v.shape, bf16),
            jax.ShapeDtypeStruct((rows, width), f32),
            jax.ShapeDtypeStruct((rows, width), f32),
        ),
        in_specs=[pl.BlockSpec(memory_space=pltpu.SMEM)] + [hbm] * 8,
        out_specs=(hbm, vmem, vmem, vmem, vmem),
        scratch_shapes=[
            pltpu.VMEM((tokens, q_width), bf16),
            pltpu.VMEM((tokens, width), bf16),
            pltpu.VMEM((tokens, width), bf16),
            pltpu.VMEM((tokens, q_width), bf16),
            pltpu.VMEM((tokens, q_width), bf16),
            pltpu.VMEM((tokens, H), f32),
            pltpu.VMEM((rows, width), bf16),
            pltpu.VMEM((rows, width), bf16),
            pltpu.VMEM((tokens, q_width), bf16),
            pltpu.VMEM((H, tokens), f32),
            pltpu.VMEM((KVH, G, tokens), f32),
            pltpu.VMEM((KVH, HD, G * tokens), f32),
            pltpu.VMEM((n * rows, 2 * width), bf16),
            pltpu.VMEM((KVH, n, rows, 2 * HD), bf16),
            pltpu.VMEM((KVH, n, rows, 2 * HD), bf16),
            pltpu.VMEM((ns, KVH, rows, 2 * HD), f32),
            dma((8,)),
            dma(()),
            dma((n,)),
            dma((n,)),
            dma((KVH, n)),
            dma((KVH, n)),
            dma((ns,)),
            dma((ns,)),
        ],
        compiler_params=pltpu.CompilerParams(
            collective_id=0, has_side_effects=True, vmem_limit_bytes=48 * 1024 * 1024
        ),
        cost_estimate=pl.CostEstimate(
            flops=2_000_000_000, bytes_accessed=5_000_000, transcendentals=1_600_000
        ),
    )(resp_lengths, resp_q, resp_k, resp_v, resp_do, resp_out, resp_lse, prompt_k, prompt_v)


def solution(mesh):
    rows = P(("sample", "prefix"), None, None)
    prompt = P("prefix", None)
    return jax.shard_map(
        body,
        mesh=mesh,
        in_specs=(rows, rows, rows, rows, rows, rows, prompt, prompt, P(("sample", "prefix"))),
        out_specs=(rows, rows, rows, prompt, prompt),
        check_vma=False,
    )
```

```python
import functools
import math

import jax
import jax.numpy as jnp
from jax import lax
from jax.experimental import pallas as pl
from jax.experimental.pallas import tpu as pltpu
from jax.sharding import PartitionSpec as P

H = 32
KVH = 4
HD = 128
G = H // KVH
MESH = pl.DeviceIdType.MESH
NT = (((1,), (1,)), ((), ()))
LOG2E = math.log2(math.e)
SCALE = HD ** (-0.5)
UB = 256


def dot(a, b):
    return jnp.dot(a, b, preferred_element_type=jnp.float32)


def dot_nt(a, b):
    return lax.dot_general(a, b, NT, preferred_element_type=jnp.float32)


def heads_to_rows(block):
    return jnp.concatenate([block[:, g * HD : (g + 1) * HD] for g in range(G)], 0)


def rows_to_lanes(block):
    return jnp.concatenate([block[g : g + 1] for g in range(G)], 1)


def part_grads(keys, values, queries, grads, lse_row, delta_row, live):
    scores = dot_nt(keys, queries)
    probs = jnp.exp2(scores * (SCALE * LOG2E) - lse_row)
    if live is not None:
        probs = jnp.where(live, probs, 0.0)
    prob_grad = dot_nt(values, grads)
    score_low = (probs * (prob_grad - delta_row)).astype(jnp.bfloat16)
    probs_low = probs.astype(jnp.bfloat16)
    dk = dot(score_low, queries) * SCALE
    dv = dot(probs_low, grads)
    return score_low, dk, dv


def kernel(
    n, ns, rows, length_hbm, q_hbm, k_hbm, v_hbm, do_hbm, out_hbm, lse_hbm, pk_hbm, pv_hbm,
    dq_hbm, dk_ref, dv_ref, pdk_ref, pdv_ref,
    length_ref, q_ref, k_ref, v_ref, do_ref, out_ref, lse_ref, dq_ref, lse_t, delta_t, score_grads,
    gathered, crossed, parts, landed, totals,
    load_sem, store_sem, gather_send, gather_recv, pass_send, pass_recv, cross_send, cross_recv,
    part_send, part_recv, total_send, total_recv,
):
    tokens = q_ref.shape[0]
    me = lax.axis_index("prefix")
    mine = lax.axis_index("sample")
    half = lax.rem(mine, 2)
    partner = {"sample": mine + 1 - 2 * half}
    heads = KVH // 2
    width = KVH * HD

    pairs = [
        (pk_hbm, gathered.at[0, 0]), (pv_hbm, gathered.at[1, 0]),
        (do_hbm.at[0], do_ref), (out_hbm.at[0], out_ref),
        (lse_hbm.at[0], lse_ref), (q_hbm.at[0], q_ref), (k_hbm.at[0], k_ref), (v_hbm.at[0], v_ref),
        (length_hbm, length_ref),
    ]
    loads = [pltpu.make_async_copy(a, b, load_sem.at[i]) for i, (a, b) in enumerate(pairs)]
    for copy in loads:
        copy.start()

    barrier = pltpu.get_barrier_semaphore()

    def greet(d, _):
        pl.semaphore_signal(
            barrier, inc=1, device_id={"prefix": lax.rem(me + d, n)}, device_id_type=MESH
        )
        return 0

    def greet_sample(d, _):
        pl.semaphore_signal(
            barrier, inc=1, device_id={"sample": lax.rem(mine + d, ns)}, device_id_type=MESH
        )
        return 0

    lax.fori_loop(1, n, greet, 0)
    lax.fori_loop(1, ns, greet_sample, 0)
    loads[0].wait()
    loads[1].wait()
    pl.semaphore_wait(barrier, n - 1 + ns - 1)

    def gather_copy(d):
        return pltpu.make_async_remote_copy(
            src_ref=gathered.at[half, 0],
            dst_ref=gathered.at[half, d],
            send_sem=gather_send.at[d],
            recv_sem=gather_recv.at[d],
            device_id={"prefix": lax.rem(me + d, n)},
            device_id_type=MESH,
        )

    def start_gather(d, _):
        gather_copy(d).start()
        return 0

    lax.fori_loop(1, n, start_gather, 0)

    for copy in loads[2:]:
        copy.wait()
    length = length_ref[0]
    key_pos = lax.broadcasted_iota(jnp.int32, (tokens, tokens), 0)
    query_pos = lax.broadcasted_iota(jnp.int32, (tokens, tokens), 1)
    causal = key_pos <= query_pos
    live_t = lax.broadcasted_iota(jnp.int32, (H, tokens), 1) < length
    lse_t[...] = jnp.where(live_t, lse_ref[...] * LOG2E, 1e30)
    prompt_rows = n * rows

    def own_step(j, _):
        cols = pl.ds(pl.multiple_of(j * G * HD, G * HD), G * HD)
        head = pl.ds(pl.multiple_of(j * HD, HD), HD)
        stat = pl.ds(pl.multiple_of(j * G, G), G)
        queries = heads_to_rows(q_ref[:, cols])
        grads = heads_to_rows(do_ref[:, cols])
        outs = heads_to_rows(out_ref[:, cols])
        product = grads.astype(jnp.float32) * outs.astype(jnp.float32)
        high = product.astype(jnp.bfloat16)
        low = (product - high.astype(jnp.float32)).astype(jnp.bfloat16)
        ones = jnp.ones((G, HD), jnp.bfloat16)
        sums = dot_nt(ones, high) + dot_nt(ones, low)
        delta_row = sums[0:1]
        for g in range(G):
            delta_t[j, g : g + 1, :] = delta_row[:, g * HD : (g + 1) * HD]
        lse_row = rows_to_lanes(lse_t[stat, :])
        live = jnp.concatenate([causal] * G, 1)
        score_low, dk, dv = part_grads(
            k_ref[:, head], v_ref[:, head], queries, grads, lse_row, delta_row, live
        )
        score_grads[j, prompt_rows:] = score_low
        dk_ref[0, :, head] = dk.astype(jnp.bfloat16)
        dv_ref[0, :, head] = dv.astype(jnp.bfloat16)
        return 0

    lax.fori_loop(0, KVH, own_step, 0)

    def pass_copy(d):
        return pltpu.make_async_remote_copy(
            src_ref=gathered.at[half, d],
            dst_ref=gathered.at[half, d],
            send_sem=pass_send.at[d],
            recv_sem=pass_recv.at[d],
            device_id=partner,
            device_id_type=MESH,
        )

    def pass_on(d, _):
        gather_copy(d).wait_recv()
        pass_copy(d).start()
        return 0

    def end_pass(d, _):
        pass_copy(d).wait_recv()
        return 0

    lax.fori_loop(1, n, pass_on, 0)
    lax.fori_loop(1, n, end_pass, 0)

    block = UB if prompt_rows % UB == 0 else prompt_rows

    def prompt_head(j, use):
        cols = pl.ds(pl.multiple_of(j * G * HD, G * HD), G * HD)
        head = pl.ds(pl.multiple_of(j * HD, HD), HD)
        stat = pl.ds(pl.multiple_of(j * G, G), G)
        queries = heads_to_rows(q_ref[:, cols])
        grads = heads_to_rows(do_ref[:, cols])
        lse_row = rows_to_lanes(lse_t[stat, :])
        delta_row = rows_to_lanes(delta_t[j])

        def block_step(b, _):
            at = pl.ds(pl.multiple_of(b * block, block), block)
            slots = pl.ds(b * (block // rows), block // rows)
            score_low, dk, dv = part_grads(
                gathered[0, slots, :, head].reshape(block, HD),
                gathered[1, slots, :, head].reshape(block, HD),
                queries, grads, lse_row, delta_row, None,
            )
            score_grads[j, at] = score_low
            use(slots, jnp.concatenate([dk, dv], 1).reshape(block // rows, rows, 2 * HD))
            return 0

        if prompt_rows == block:
            block_step(0, 0)
        else:
            lax.fori_loop(0, prompt_rows // block, block_step, 0)

    def cross_copy(i):
        return pltpu.make_async_remote_copy(
            src_ref=crossed.at[0, i],
            dst_ref=crossed.at[1, i],
            send_sem=cross_send.at[i],
            recv_sem=cross_recv.at[i],
            device_id=partner,
            device_id_type=MESH,
        )

    def cross_step(i, _):
        def use(slots, both):
            crossed[0, i, slots] = both

        prompt_head((1 - half) * heads + i, use)
        cross_copy(i).start()
        return 0

    lax.fori_loop(0, heads, cross_step, 0)

    def part_copy(i, d):
        return pltpu.make_async_remote_copy(
            src_ref=parts.at[i, d],
            dst_ref=landed.at[i, d],
            send_sem=part_send.at[i, d],
            recv_sem=part_recv.at[i, d],
            device_id={"prefix": lax.rem(me + n - d, n)},
            device_id_type=MESH,
        )

    def part_step(i, _):
        cross_copy(i).wait_recv()

        def use(slots, both):
            parts[i, slots] = (both + crossed[1, i, slots]).astype(jnp.bfloat16)

        prompt_head(half * heads + i, use)

        def start_part(d, _):
            part_copy(i, d).start()
            return 0

        lax.fori_loop(1, n, start_part, 0)
        return 0

    lax.fori_loop(0, heads, part_step, 0)

    def query_step(j, _):
        head = pl.ds(pl.multiple_of(j * HD, HD), HD)
        keys = jnp.concatenate(
            [gathered[0, :, :, head].reshape(prompt_rows, HD), k_ref[:, head]], 0
        )
        dq_t = (dot(keys.T, score_grads[j]) * SCALE).astype(jnp.bfloat16)
        for g in range(G):
            at = pl.ds(pl.multiple_of((j * G + g) * HD, HD), HD)
            dq_ref[:, at] = dq_t[:, g * HD : (g + 1) * HD].T
        return 0

    lax.fori_loop(0, KVH, query_step, 0)
    store = pltpu.make_async_copy(dq_ref, dq_hbm.at[0], store_sem)
    store.start()

    def end_sends(d, _):
        gather_copy(d).wait_send()
        pass_copy(d).wait_send()
        return 0

    lax.fori_loop(1, n, end_sends, 0)
    for i in range(heads):
        cross_copy(i).wait_send()

    def sum_step(i, _):
        def wait_part(d, _):
            part_copy(i, d).wait()
            return 0

        lax.fori_loop(1, n, wait_part, 0)
        others = jnp.sum(landed[i, 1:].astype(jnp.float32), 0)
        totals[mine, i] = others + parts[i, 0].astype(jnp.float32)
        return 0

    lax.fori_loop(0, heads, sum_step, 0)

    def total_copy(d):
        return pltpu.make_async_remote_copy(
            src_ref=totals.at[mine],
            dst_ref=totals.at[mine],
            send_sem=total_send.at[d],
            recv_sem=total_recv.at[d],
            device_id={"sample": lax.rem(mine + d, ns)},
            device_id_type=MESH,
        )

    for d in range(1, ns):
        total_copy(d).start()
    for d in range(1, ns):
        total_copy(d).wait()
    for j in range(KVH):
        both = totals[j // heads, j % heads]
        for s in range(2 + j // heads, ns, 2):
            both = both + totals[s, j % heads]
        pdk_ref[:, j * HD : (j + 1) * HD] = both[:, :HD]
        pdv_ref[:, j * HD : (j + 1) * HD] = both[:, HD:]
    store.wait()


def store_kernel(*refs):
    *arrays, sem = refs
    count = len(arrays) // 2
    copies = [
        pltpu.make_async_copy(arrays[i], arrays[count + i], sem.at[i]) for i in range(count)
    ]
    for copy in copies:
        copy.start()
    for copy in copies:
        copy.wait()


def body(resp_q, resp_k, resp_v, resp_do, resp_out, resp_lse, prompt_k, prompt_v, resp_lengths):
    n = lax.axis_size("prefix")
    ns = lax.axis_size("sample")
    rows, width = prompt_k.shape
    _, tokens, q_width = resp_q.shape
    bf16, f32 = jnp.bfloat16, jnp.float32
    heads = KVH // 2
    vmem = pl.BlockSpec(memory_space=pltpu.VMEM)
    hbm = pl.BlockSpec(memory_space=pltpu.HBM)
    free = pl.BlockSpec(memory_space=pl.ANY)
    dma = pltpu.SemaphoreType.DMA
    out_shape = (
        jax.ShapeDtypeStruct(resp_q.shape, bf16),
        jax.ShapeDtypeStruct(resp_k.shape, bf16),
        jax.ShapeDtypeStruct(resp_v.shape, bf16),
        jax.ShapeDtypeStruct((rows, width), f32),
        jax.ShapeDtypeStruct((rows, width), f32),
    )
    results = pl.pallas_call(
        functools.partial(kernel, n, ns, rows),
        out_shape=out_shape,
        in_specs=[hbm] * 9,
        out_specs=(free, vmem, vmem, vmem, vmem),
        scratch_shapes=[
            pltpu.SMEM((1,), jnp.int32),
            pltpu.VMEM((tokens, q_width), bf16),
            pltpu.VMEM((tokens, width), bf16),
            pltpu.VMEM((tokens, width), bf16),
            pltpu.VMEM((tokens, q_width), bf16),
            pltpu.VMEM((tokens, q_width), bf16),
            pltpu.VMEM((H, tokens), f32),
            pltpu.VMEM((tokens, q_width), bf16),
            pltpu.VMEM((H, tokens), f32),
            pltpu.VMEM((KVH, G, tokens), f32),
            pltpu.VMEM((KVH, n * rows + tokens, G * tokens), bf16),
            pltpu.VMEM((2, n, rows, width), bf16),
            pltpu.VMEM((2, heads, n, rows, 2 * HD), f32),
            pltpu.VMEM((heads, n, rows, 2 * HD), bf16),
            pltpu.VMEM((heads, n, rows, 2 * HD), bf16),
            pltpu.VMEM((ns, heads, rows, 2 * HD), f32),
            dma((9,)),
            dma(()),
            dma((n,)),
            dma((n,)),
            dma((n,)),
            dma((n,)),
            dma((heads,)),
            dma((heads,)),
            dma((heads, n)),
            dma((heads, n)),
            dma((ns,)),
            dma((ns,)),
        ],
        compiler_params=pltpu.CompilerParams(
            collective_id=0, has_side_effects=True, vmem_limit_bytes=63 * 1024 * 1024
        ),
        cost_estimate=pl.CostEstimate(
            flops=2_000_000_000, bytes_accessed=5_000_000, transcendentals=1_600_000
        ),
    )(
        resp_lengths, resp_q, resp_k, resp_v, resp_do, resp_out, jnp.swapaxes(resp_lse, 1, 2),
        prompt_k, prompt_v,
    )
    return pl.pallas_call(
        store_kernel,
        out_shape=out_shape,
        in_specs=[free] * 5,
        out_specs=(hbm,) * 5,
        scratch_shapes=[dma((5,))],
        compiler_params=pltpu.CompilerParams(vmem_limit_bytes=63 * 1024 * 1024),
    )(*results)


def solution(mesh):
    rows = P(("sample", "prefix"), None, None)
    prompt = P("prefix", None)
    return jax.shard_map(
        body,
        mesh=mesh,
        in_specs=(rows, rows, rows, rows, rows, rows, prompt, prompt, P(("sample", "prefix"))),
        out_specs=(rows, rows, rows, prompt, prompt),
        check_vma=False,
    )
```

```python
import functools
import math

import jax
import jax.numpy as jnp
from jax import lax
from jax.experimental import pallas as pl
from jax.experimental.pallas import tpu as pltpu
from jax.sharding import PartitionSpec as P

H = 32
KVH = 4
HD = 128
G = H // KVH
MESH = pl.DeviceIdType.MESH
NT = (((1,), (1,)), ((), ()))
LOG2E = math.log2(math.e)
SCALE = HD ** (-0.5)
UB = 256


def dot(a, b):
    return jnp.dot(a, b, preferred_element_type=jnp.float32)


def dot_nt(a, b):
    return lax.dot_general(a, b, NT, preferred_element_type=jnp.float32)


def head_pair(ref, j):
    def read(first):
        at = [pl.ds(pl.multiple_of((j * G + g) * HD, HD), HD) for g in (first, first + 1)]
        return jnp.concatenate([ref[:, cols] for cols in at], 0)

    return read


def rows_to_lanes(block):
    return jnp.concatenate([block[g : g + 1] for g in range(G)], 1)


def part_grads(keys, values, queries, grads, lse_row, delta_row, live, keep):
    dk = dv = None
    for first in range(0, G, 2):
        chunk = slice(first * lse_row.shape[1] // G, (first + 2) * lse_row.shape[1] // G)
        query, grad = queries(first), grads(first)
        scores = dot_nt(keys, query)
        probs = jnp.exp2(scores * (SCALE * LOG2E) - lse_row[:, chunk])
        if live is not None:
            probs = jnp.where(live, probs, 0.0)
        prob_grad = dot_nt(values, grad)
        score_low = (probs * (prob_grad - delta_row[:, chunk])).astype(jnp.bfloat16)
        keep(chunk, score_low)
        dk_term = dot(score_low, query)
        dv_term = dot(probs.astype(jnp.bfloat16), grad)
        dk = dk_term if dk is None else dk + dk_term
        dv = dv_term if dv is None else dv + dv_term
    return dk * SCALE, dv


def kernel(
    n, ns, rows, length_hbm, q_hbm, k_hbm, v_hbm, do_hbm, out_hbm, lse_hbm, pk_hbm, pv_hbm,
    dq_hbm, dk_hbm, dv_hbm, pdk_ref, pdv_ref,
    dk_ref, dv_ref, length_ref, q_ref, k_ref, v_ref, do_ref, out_ref, lse_ref, dq_ref, lse_t, delta_t, score_grads,
    gathered, crossed, parts, landed, totals,
    load_sem, store_sem, gather_send, gather_recv, pass_send, pass_recv, cross_send, cross_recv,
    part_send, part_recv, total_send, total_recv,
):
    tokens = q_ref.shape[0]
    me = lax.axis_index("prefix")
    mine = lax.axis_index("sample")
    half = lax.rem(mine, 2)
    partner = {"sample": mine + 1 - 2 * half}
    heads = KVH // 2
    width = KVH * HD

    pairs = [
        (pk_hbm, gathered.at[0, 0]), (pv_hbm, gathered.at[1, 0]),
        (do_hbm.at[0], do_ref), (out_hbm.at[0], out_ref),
        (lse_hbm.at[0], lse_ref), (q_hbm.at[0], q_ref), (k_hbm.at[0], k_ref), (v_hbm.at[0], v_ref),
        (length_hbm, length_ref),
    ]
    loads = [pltpu.make_async_copy(a, b, load_sem.at[i]) for i, (a, b) in enumerate(pairs)]
    loads[0].start()
    loads[1].start()

    barrier = pltpu.get_barrier_semaphore()

    def greet(d, _):
        pl.semaphore_signal(
            barrier, inc=1, device_id={"prefix": lax.rem(me + d, n)}, device_id_type=MESH
        )
        return 0

    def greet_sample(d, _):
        pl.semaphore_signal(
            barrier, inc=1, device_id={"sample": lax.rem(mine + d, ns)}, device_id_type=MESH
        )
        return 0

    lax.fori_loop(1, n, greet, 0)
    lax.fori_loop(1, ns, greet_sample, 0)
    for copy in loads[2:]:
        copy.start()
    loads[0].wait()
    loads[1].wait()
    pl.semaphore_wait(barrier, n - 1 + ns - 1)

    def gather_copy(d):
        return pltpu.make_async_remote_copy(
            src_ref=gathered.at[half, 0],
            dst_ref=gathered.at[half, d],
            send_sem=gather_send.at[d],
            recv_sem=gather_recv.at[d],
            device_id={"prefix": lax.rem(me + d, n)},
            device_id_type=MESH,
        )

    def start_gather(d, _):
        gather_copy(d).start()
        return 0

    lax.fori_loop(1, n, start_gather, 0)

    for copy in loads[2:]:
        copy.wait()
    length = length_ref[0]
    key_pos = lax.broadcasted_iota(jnp.int32, (tokens, tokens), 0)
    query_pos = lax.broadcasted_iota(jnp.int32, (tokens, tokens), 1)
    causal = key_pos <= query_pos
    live_t = lax.broadcasted_iota(jnp.int32, (H, tokens), 1) < length
    lse_t[...] = jnp.where(live_t, lse_ref[...] * LOG2E, 1e30)
    prompt_rows = n * rows

    def own_step(j, _):
        head = pl.ds(pl.multiple_of(j * HD, HD), HD)
        stat = pl.ds(pl.multiple_of(j * G, G), G)
        ones = jnp.ones((G, HD), jnp.bfloat16)
        sums = []
        for first in range(0, G, 2):
            grads = head_pair(do_ref, j)(first).astype(jnp.float32)
            product = grads * head_pair(out_ref, j)(first).astype(jnp.float32)
            high = product.astype(jnp.bfloat16)
            low = (product - high.astype(jnp.float32)).astype(jnp.bfloat16)
            sums.append((dot_nt(ones, high) + dot_nt(ones, low))[0:1])
        delta_row = jnp.concatenate(sums, 1)
        delta_t[j] = delta_row
        lse_row = rows_to_lanes(lse_t[stat, :])

        def keep(chunk, score_low):
            score_grads[j, prompt_rows:, chunk] = score_low

        dk, dv = part_grads(
            k_ref[:, head], v_ref[:, head], head_pair(q_ref, j), head_pair(do_ref, j),
            lse_row, delta_row, jnp.concatenate([causal] * 2, 1), keep,
        )
        dk_ref[:, head] = dk.astype(jnp.bfloat16)
        dv_ref[:, head] = dv.astype(jnp.bfloat16)
        return 0

    lax.fori_loop(0, KVH, own_step, 0)
    stores = [
        pltpu.make_async_copy(dk_ref, dk_hbm.at[0], store_sem.at[0]),
        pltpu.make_async_copy(dv_ref, dv_hbm.at[0], store_sem.at[1]),
        pltpu.make_async_copy(dq_ref, dq_hbm.at[0], store_sem.at[2]),
    ]
    stores[0].start()
    stores[1].start()

    def pass_copy(d):
        return pltpu.make_async_remote_copy(
            src_ref=gathered.at[half, d],
            dst_ref=gathered.at[half, d],
            send_sem=pass_send.at[d],
            recv_sem=pass_recv.at[d],
            device_id=partner,
            device_id_type=MESH,
        )

    def pass_on(d, _):
        gather_copy(d).wait_recv()
        pass_copy(d).start()
        return 0

    def end_pass(d, _):
        pass_copy(d).wait_recv()
        return 0

    lax.fori_loop(1, n, pass_on, 0)
    lax.fori_loop(1, n, end_pass, 0)

    block = UB if prompt_rows % UB == 0 else prompt_rows

    def prompt_head(j, use):
        head = pl.ds(pl.multiple_of(j * HD, HD), HD)
        stat = pl.ds(pl.multiple_of(j * G, G), G)
        lse_row = rows_to_lanes(lse_t[stat, :])
        delta_row = delta_t[j]

        def block_step(b, _):
            at = pl.ds(pl.multiple_of(b * block, block), block)
            slots = pl.ds(b * (block // rows), block // rows)

            def keep(chunk, score_low):
                score_grads[j, at, chunk] = score_low

            dk, dv = part_grads(
                gathered[0, slots, :, head].reshape(block, HD),
                gathered[1, slots, :, head].reshape(block, HD),
                head_pair(q_ref, j), head_pair(do_ref, j), lse_row, delta_row, None, keep,
            )
            use(slots, jnp.concatenate([dk, dv], 1).reshape(block // rows, rows, 2 * HD))
            return 0

        if prompt_rows == block:
            block_step(0, 0)
        else:
            lax.fori_loop(0, prompt_rows // block, block_step, 0)

    def cross_copy(i):
        return pltpu.make_async_remote_copy(
            src_ref=crossed.at[0, i],
            dst_ref=crossed.at[1, i],
            send_sem=cross_send.at[i],
            recv_sem=cross_recv.at[i],
            device_id=partner,
            device_id_type=MESH,
        )

    def cross_step(i, _):
        def use(slots, both):
            crossed[0, i, slots] = both

        prompt_head((1 - half) * heads + i, use)
        cross_copy(i).start()
        return 0

    lax.fori_loop(0, heads, cross_step, 0)

    def part_copy(i, d):
        return pltpu.make_async_remote_copy(
            src_ref=parts.at[i, d],
            dst_ref=landed.at[i, d],
            send_sem=part_send.at[i, d],
            recv_sem=part_recv.at[i, d],
            device_id={"prefix": lax.rem(me + n - d, n)},
            device_id_type=MESH,
        )

    def part_step(i, _):
        cross_copy(i).wait_recv()

        def use(slots, both):
            parts[i, slots] = (both + crossed[1, i, slots]).astype(jnp.bfloat16)

        prompt_head(half * heads + i, use)

        def start_part(d, _):
            part_copy(i, d).start()
            return 0

        lax.fori_loop(1, n, start_part, 0)
        return 0

    lax.fori_loop(0, heads, part_step, 0)

    def query_step(j, _):
        head = pl.ds(pl.multiple_of(j * HD, HD), HD)
        keys = jnp.concatenate(
            [gathered[0, :, :, head].reshape(prompt_rows, HD), k_ref[:, head]], 0
        )
        dq_t = (dot(keys.T, score_grads[j]) * SCALE).astype(jnp.bfloat16)
        for g in range(G):
            at = pl.ds(pl.multiple_of((j * G + g) * HD, HD), HD)
            dq_ref[:, at] = dq_t[:, g * HD : (g + 1) * HD].T
        return 0

    lax.fori_loop(0, KVH, query_step, 0)
    stores[2].start()

    def end_sends(d, _):
        gather_copy(d).wait_send()
        pass_copy(d).wait_send()
        return 0

    lax.fori_loop(1, n, end_sends, 0)
    for i in range(heads):
        cross_copy(i).wait_send()

    def sum_step(i, _):
        def wait_part(d, _):
            part_copy(i, d).wait()
            return 0

        lax.fori_loop(1, n, wait_part, 0)
        others = jnp.sum(landed[i, 1:].astype(jnp.float32), 0)
        totals[mine, i] = others + parts[i, 0].astype(jnp.float32)
        return 0

    lax.fori_loop(0, heads, sum_step, 0)

    def total_copy(d):
        return pltpu.make_async_remote_copy(
            src_ref=totals.at[mine],
            dst_ref=totals.at[mine],
            send_sem=total_send.at[d],
            recv_sem=total_recv.at[d],
            device_id={"sample": lax.rem(mine + d, ns)},
            device_id_type=MESH,
        )

    for d in range(1, ns):
        total_copy(d).start()
    for d in range(1, ns):
        total_copy(d).wait()
    for j in range(KVH):
        both = totals[j // heads, j % heads]
        for s in range(2 + j // heads, ns, 2):
            both = both + totals[s, j % heads]
        pdk_ref[:, j * HD : (j + 1) * HD] = both[:, :HD]
        pdv_ref[:, j * HD : (j + 1) * HD] = both[:, HD:]
    for store in stores:
        store.wait()


def store_kernel(*refs):
    *arrays, sem = refs
    count = len(arrays) // 2
    copies = [
        pltpu.make_async_copy(arrays[i], arrays[count + i], sem.at[i]) for i in range(count)
    ]
    for copy in copies:
        copy.start()
    for copy in copies:
        copy.wait()


def body(resp_q, resp_k, resp_v, resp_do, resp_out, resp_lse, prompt_k, prompt_v, resp_lengths):
    n = lax.axis_size("prefix")
    ns = lax.axis_size("sample")
    rows, width = prompt_k.shape
    _, tokens, q_width = resp_q.shape
    bf16, f32 = jnp.bfloat16, jnp.float32
    heads = KVH // 2
    vmem = pl.BlockSpec(memory_space=pltpu.VMEM)
    hbm = pl.BlockSpec(memory_space=pltpu.HBM)
    free = pl.BlockSpec(memory_space=pl.ANY)
    dma = pltpu.SemaphoreType.DMA
    out_shape = (
        jax.ShapeDtypeStruct(resp_q.shape, bf16),
        jax.ShapeDtypeStruct(resp_k.shape, bf16),
        jax.ShapeDtypeStruct(resp_v.shape, bf16),
        jax.ShapeDtypeStruct((rows, width), f32),
        jax.ShapeDtypeStruct((rows, width), f32),
    )
    args = (
        resp_lengths, resp_q, resp_k, resp_v, resp_do, resp_out, jnp.swapaxes(resp_lse, 1, 2),
        prompt_k, prompt_v,
    )
    args = args[:1] + tuple(pltpu.with_memory_space_constraint(arg, pltpu.HBM) for arg in args[1:])
    results = pl.pallas_call(
        functools.partial(kernel, n, ns, rows),
        out_shape=tuple(pltpu.VMEM(o.shape, o.dtype) for o in out_shape),
        in_specs=[hbm] * 9,
        out_specs=(free, free, free, vmem, vmem),
        scratch_shapes=[
            pltpu.VMEM((tokens, width), bf16),
            pltpu.VMEM((tokens, width), bf16),
            pltpu.SMEM((1,), jnp.int32),
            pltpu.VMEM((tokens, q_width), bf16),
            pltpu.VMEM((tokens, width), bf16),
            pltpu.VMEM((tokens, width), bf16),
            pltpu.VMEM((tokens, q_width), bf16),
            pltpu.VMEM((tokens, q_width), bf16),
            pltpu.VMEM((H, tokens), f32),
            pltpu.VMEM((tokens, q_width), bf16),
            pltpu.VMEM((H, tokens), f32),
            pltpu.VMEM((KVH, 1, G * tokens), f32),
            pltpu.VMEM((KVH, n * rows + tokens, G * tokens), bf16),
            pltpu.VMEM((2, n, rows, width), bf16),
            pltpu.VMEM((2, heads, n, rows, 2 * HD), f32),
            pltpu.VMEM((heads, n, rows, 2 * HD), bf16),
            pltpu.VMEM((heads, n, rows, 2 * HD), bf16),
            pltpu.VMEM((ns, heads, rows, 2 * HD), f32),
            dma((9,)),
            dma((3,)),
            dma((n,)),
            dma((n,)),
            dma((n,)),
            dma((n,)),
            dma((heads,)),
            dma((heads,)),
            dma((heads, n)),
            dma((heads, n)),
            dma((ns,)),
            dma((ns,)),
        ],
        compiler_params=pltpu.CompilerParams(
            collective_id=0, has_side_effects=True, vmem_limit_bytes=48 * 1024 * 1024
        ),
        cost_estimate=pl.CostEstimate(
            flops=2_000_000_000, bytes_accessed=5_000_000, transcendentals=1_600_000
        ),
    )(*args)
    return pl.pallas_call(
        store_kernel,
        out_shape=out_shape,
        in_specs=[free] * 5,
        out_specs=(hbm,) * 5,
        scratch_shapes=[dma((5,))],
    )(*results)


def solution(mesh):
    rows = P(("sample", "prefix"), None, None)
    prompt = P("prefix", None)
    return jax.shard_map(
        body,
        mesh=mesh,
        in_specs=(rows, rows, rows, rows, rows, rows, prompt, prompt, P(("sample", "prefix"))),
        out_specs=(rows, rows, rows, prompt, prompt),
        check_vma=False,
    )
```

```python
import functools
import math

import jax
import jax.numpy as jnp
from jax import lax
from jax.experimental import pallas as pl
from jax.experimental.pallas import tpu as pltpu
from jax.sharding import PartitionSpec as P

H = 32
KVH = 4
HD = 128
G = H // KVH
MESH = pl.DeviceIdType.MESH
NT = (((1,), (1,)), ((), ()))
LOG2E = math.log2(math.e)
SCALE = HD ** (-0.5)
UB = 256


def dot(a, b):
    return jnp.dot(a, b, preferred_element_type=jnp.float32)


def dot_nt(a, b):
    return lax.dot_general(a, b, NT, preferred_element_type=jnp.float32)


def head_pair(ref, j):
    def read(first):
        at = [pl.ds(pl.multiple_of((j * G + g) * HD, HD), HD) for g in (first, first + 1)]
        return jnp.concatenate([ref[:, cols] for cols in at], 0)

    return read


def rows_to_lanes(block):
    return jnp.concatenate([block[g : g + 1] for g in range(G)], 1)


def part_grads(keys, values, queries, grads, lse_row, delta_row, live, keep):
    dk = dv = None
    for first in range(0, G, 2):
        chunk = slice(first * lse_row.shape[1] // G, (first + 2) * lse_row.shape[1] // G)
        query, grad = queries(first), grads(first)
        scores = dot_nt(keys, query)
        probs = jnp.exp2(scores * (SCALE * LOG2E) - lse_row[:, chunk])
        if live is not None:
            probs = jnp.where(live, probs, 0.0)
        prob_grad = dot_nt(values, grad)
        score_low = (probs * (prob_grad - delta_row[:, chunk])).astype(jnp.bfloat16)
        keep(chunk, score_low)
        dk_term = dot(score_low, query)
        dv_term = dot(probs.astype(jnp.bfloat16), grad)
        dk = dk_term if dk is None else dk + dk_term
        dv = dv_term if dv is None else dv + dv_term
    return dk * SCALE, dv


def kernel(
    n, ns, rows, length_hbm, q_hbm, k_hbm, v_hbm, do_hbm, out_hbm, lse_hbm, pk_hbm, pv_hbm,
    dq_hbm, dk_hbm, dv_hbm, pdk_ref, pdv_ref,
    dk_ref, dv_ref, length_ref, q_ref, k_ref, v_ref, do_ref, out_ref, lse_ref, dq_ref, lse_t, delta_t, score_grads,
    gathered, crossed, parts, landed, totals,
    load_sem, store_sem, gather_send, gather_recv, pass_send, pass_recv, cross_send, cross_recv,
    part_send, part_recv, total_send, total_recv,
):
    tokens = q_ref.shape[0]
    me = lax.axis_index("prefix")
    mine = lax.axis_index("sample")
    half = lax.rem(mine, 2)
    partner = {"sample": mine + 1 - 2 * half}
    heads = KVH // 2
    width = KVH * HD

    pairs = [
        (pk_hbm, gathered.at[0, 0]), (pv_hbm, gathered.at[1, 0]),
        (do_hbm.at[0], do_ref), (out_hbm.at[0], out_ref),
        (lse_hbm.at[0], lse_ref), (q_hbm.at[0], q_ref), (k_hbm.at[0], k_ref), (v_hbm.at[0], v_ref),
        (length_hbm, length_ref),
    ]
    loads = [pltpu.make_async_copy(a, b, load_sem.at[i]) for i, (a, b) in enumerate(pairs)]

    barrier = pltpu.get_barrier_semaphore()

    def greet(d, _):
        pl.semaphore_signal(
            barrier, inc=1, device_id={"prefix": lax.rem(me + d, n)}, device_id_type=MESH
        )
        return 0

    def greet_sample(d, _):
        pl.semaphore_signal(
            barrier, inc=1, device_id={"sample": lax.rem(mine + d, ns)}, device_id_type=MESH
        )
        return 0

    lax.fori_loop(1, n, greet, 0)
    lax.fori_loop(1, ns, greet_sample, 0)
    for copy in loads:
        copy.start()
    pl.semaphore_wait(barrier, n - 1 + ns - 1)

    def gather_copy(d, source=pk_hbm):
        return pltpu.make_async_remote_copy(
            src_ref=source,
            dst_ref=gathered.at[half, d],
            send_sem=gather_send.at[d],
            recv_sem=gather_recv.at[d],
            device_id={"prefix": lax.rem(me + d, n)},
            device_id_type=MESH,
        )

    for which, source in enumerate((pk_hbm, pv_hbm)):

        @pl.when(half == which)
        def _():
            def start_gather(d, _):
                gather_copy(d, source).start()
                return 0

            lax.fori_loop(1, n, start_gather, 0)

    for copy in loads:
        copy.wait()
    length = length_ref[0]
    key_pos = lax.broadcasted_iota(jnp.int32, (tokens, tokens), 0)
    query_pos = lax.broadcasted_iota(jnp.int32, (tokens, tokens), 1)
    causal = key_pos <= query_pos
    live_t = lax.broadcasted_iota(jnp.int32, (H, tokens), 1) < length
    lse_t[...] = jnp.where(live_t, lse_ref[...] * LOG2E, 1e30)
    lanes = lax.broadcasted_iota(jnp.int32, (tokens, HD), 1)
    deltas = jnp.zeros((tokens, HD), jnp.float32)
    for h in range(H):
        at = slice(h * HD, (h + 1) * HD)
        product = do_ref[:, at].astype(jnp.float32) * out_ref[:, at].astype(jnp.float32)
        deltas = jnp.where(lanes == h, jnp.sum(product, 1, keepdims=True), deltas)
    delta_t[...] = deltas.T
    prompt_rows = n * rows

    def own_step(j, _):
        head = pl.ds(pl.multiple_of(j * HD, HD), HD)
        stat = pl.ds(pl.multiple_of(j * G, G), G)
        delta_row = rows_to_lanes(delta_t[stat, :])
        lse_row = rows_to_lanes(lse_t[stat, :])

        def keep(chunk, score_low):
            score_grads[j, prompt_rows:, chunk] = score_low

        dk, dv = part_grads(
            k_ref[:, head], v_ref[:, head], head_pair(q_ref, j), head_pair(do_ref, j),
            lse_row, delta_row, jnp.concatenate([causal] * 2, 1), keep,
        )
        dk_ref[:, head] = dk.astype(jnp.bfloat16)
        dv_ref[:, head] = dv.astype(jnp.bfloat16)
        return 0

    lax.fori_loop(0, KVH, own_step, 0)
    stores = [
        pltpu.make_async_copy(dk_ref, dk_hbm.at[0], store_sem.at[0]),
        pltpu.make_async_copy(dv_ref, dv_hbm.at[0], store_sem.at[1]),
        pltpu.make_async_copy(dq_ref, dq_hbm.at[0], store_sem.at[2]),
    ]
    stores[0].start()
    stores[1].start()

    def pass_copy(d):
        return pltpu.make_async_remote_copy(
            src_ref=gathered.at[half, d],
            dst_ref=gathered.at[half, d],
            send_sem=pass_send.at[d],
            recv_sem=pass_recv.at[d],
            device_id=partner,
            device_id_type=MESH,
        )

    def pass_on(d, _):
        gather_copy(d).wait_recv()
        pass_copy(d).start()
        return 0

    def end_pass(d, _):
        pass_copy(d).wait_recv()
        return 0

    lax.fori_loop(1, n, pass_on, 0)
    lax.fori_loop(1, n, end_pass, 0)

    block = UB if prompt_rows % UB == 0 else prompt_rows

    def prompt_head(j, use):
        head = pl.ds(pl.multiple_of(j * HD, HD), HD)
        stat = pl.ds(pl.multiple_of(j * G, G), G)
        lse_row = rows_to_lanes(lse_t[stat, :])
        delta_row = rows_to_lanes(delta_t[stat, :])

        def block_step(b, _):
            at = pl.ds(pl.multiple_of(b * block, block), block)
            slots = pl.ds(b * (block // rows), block // rows)

            def keep(chunk, score_low):
                score_grads[j, at, chunk] = score_low

            dk, dv = part_grads(
                gathered[0, slots, :, head].reshape(block, HD),
                gathered[1, slots, :, head].reshape(block, HD),
                head_pair(q_ref, j), head_pair(do_ref, j), lse_row, delta_row, None, keep,
            )
            use(slots, jnp.concatenate([dk, dv], 1).reshape(block // rows, rows, 2 * HD))
            return 0

        if prompt_rows == block:
            block_step(0, 0)
        else:
            lax.fori_loop(0, prompt_rows // block, block_step, 0)

    def cross_copy(i):
        return pltpu.make_async_remote_copy(
            src_ref=crossed.at[0, i],
            dst_ref=crossed.at[1, i],
            send_sem=cross_send.at[i],
            recv_sem=cross_recv.at[i],
            device_id=partner,
            device_id_type=MESH,
        )

    def cross_step(i, _):
        def use(slots, both):
            crossed[0, i, slots] = both

        prompt_head((1 - half) * heads + i, use)
        cross_copy(i).start()
        return 0

    lax.fori_loop(0, heads, cross_step, 0)

    def part_copy(i, d):
        return pltpu.make_async_remote_copy(
            src_ref=parts.at[i, d],
            dst_ref=landed.at[i, d],
            send_sem=part_send.at[i, d],
            recv_sem=part_recv.at[i, d],
            device_id={"prefix": lax.rem(me + n - d, n)},
            device_id_type=MESH,
        )

    def part_step(i, _):
        cross_copy(i).wait_recv()

        def use(slots, both):
            parts[i, slots] = (both + crossed[1, i, slots]).astype(jnp.bfloat16)

        prompt_head(half * heads + i, use)

        def start_part(d, _):
            part_copy(i, d).start()
            return 0

        lax.fori_loop(1, n, start_part, 0)
        return 0

    lax.fori_loop(0, heads, part_step, 0)

    def query_step(j, _):
        head = pl.ds(pl.multiple_of(j * HD, HD), HD)
        keys = jnp.concatenate(
            [gathered[0, :, :, head].reshape(prompt_rows, HD), k_ref[:, head]], 0
        )
        dq_t = (dot(keys.T, score_grads[j]) * SCALE).astype(jnp.bfloat16)
        for g in range(G):
            at = pl.ds(pl.multiple_of((j * G + g) * HD, HD), HD)
            dq_ref[:, at] = dq_t[:, g * HD : (g + 1) * HD].T
        return 0

    lax.fori_loop(0, KVH, query_step, 0)
    stores[2].start()

    def end_sends(d, _):
        gather_copy(d).wait_send()
        pass_copy(d).wait_send()
        return 0

    lax.fori_loop(1, n, end_sends, 0)
    for i in range(heads):
        cross_copy(i).wait_send()

    def sum_step(i, _):
        def wait_part(d, _):
            part_copy(i, d).wait()
            return 0

        lax.fori_loop(1, n, wait_part, 0)
        others = jnp.sum(landed[i, 1:].astype(jnp.float32), 0)
        totals[mine, i] = others + parts[i, 0].astype(jnp.float32)
        return 0

    lax.fori_loop(0, heads, sum_step, 0)

    def total_copy(d):
        return pltpu.make_async_remote_copy(
            src_ref=totals.at[mine],
            dst_ref=totals.at[mine],
            send_sem=total_send.at[d],
            recv_sem=total_recv.at[d],
            device_id={"sample": lax.rem(mine + d, ns)},
            device_id_type=MESH,
        )

    for d in range(1, ns):
        total_copy(d).start()
    for d in range(1, ns):
        total_copy(d).wait()
    for j in range(KVH):
        both = totals[j // heads, j % heads]
        for s in range(2 + j // heads, ns, 2):
            both = both + totals[s, j % heads]
        pdk_ref[:, j * HD : (j + 1) * HD] = both[:, :HD]
        pdv_ref[:, j * HD : (j + 1) * HD] = both[:, HD:]
    for store in stores:
        store.wait()


def store_kernel(*refs):
    *arrays, sem = refs
    count = len(arrays) // 2
    copies = [
        pltpu.make_async_copy(arrays[i], arrays[count + i], sem.at[i]) for i in range(count)
    ]
    for copy in copies:
        copy.start()
    for copy in copies:
        copy.wait()


def body(resp_q, resp_k, resp_v, resp_do, resp_out, resp_lse, prompt_k, prompt_v, resp_lengths):
    n = lax.axis_size("prefix")
    ns = lax.axis_size("sample")
    rows, width = prompt_k.shape
    _, tokens, q_width = resp_q.shape
    bf16, f32 = jnp.bfloat16, jnp.float32
    heads = KVH // 2
    vmem = pl.BlockSpec(memory_space=pltpu.VMEM)
    hbm = pl.BlockSpec(memory_space=pltpu.HBM)
    free = pl.BlockSpec(memory_space=pl.ANY)
    dma = pltpu.SemaphoreType.DMA
    out_shape = (
        jax.ShapeDtypeStruct(resp_q.shape, bf16),
        jax.ShapeDtypeStruct(resp_k.shape, bf16),
        jax.ShapeDtypeStruct(resp_v.shape, bf16),
        jax.ShapeDtypeStruct((rows, width), f32),
        jax.ShapeDtypeStruct((rows, width), f32),
    )
    args = (
        resp_lengths, resp_q, resp_k, resp_v, resp_do, resp_out, jnp.swapaxes(resp_lse, 1, 2),
        prompt_k, prompt_v,
    )
    args = args[:1] + tuple(pltpu.with_memory_space_constraint(arg, pltpu.HBM) for arg in args[1:])
    results = pl.pallas_call(
        functools.partial(kernel, n, ns, rows),
        out_shape=tuple(pltpu.VMEM(o.shape, o.dtype) for o in out_shape),
        in_specs=[hbm] * 9,
        out_specs=(free, free, free, vmem, vmem),
        scratch_shapes=[
            pltpu.VMEM((tokens, width), bf16),
            pltpu.VMEM((tokens, width), bf16),
            pltpu.SMEM((1,), jnp.int32),
            pltpu.VMEM((tokens, q_width), bf16),
            pltpu.VMEM((tokens, width), bf16),
            pltpu.VMEM((tokens, width), bf16),
            pltpu.VMEM((tokens, q_width), bf16),
            pltpu.VMEM((tokens, q_width), bf16),
            pltpu.VMEM((H, tokens), f32),
            pltpu.VMEM((tokens, q_width), bf16),
            pltpu.VMEM((H, tokens), f32),
            pltpu.VMEM((HD, tokens), f32),
            pltpu.VMEM((KVH, n * rows + tokens, G * tokens), bf16),
            pltpu.VMEM((2, n, rows, width), bf16),
            pltpu.VMEM((2, heads, n, rows, 2 * HD), f32),
            pltpu.VMEM((heads, n, rows, 2 * HD), bf16),
            pltpu.VMEM((heads, n, rows, 2 * HD), bf16),
            pltpu.VMEM((ns, heads, rows, 2 * HD), f32),
            dma((9,)),
            dma((3,)),
            dma((n,)),
            dma((n,)),
            dma((n,)),
            dma((n,)),
            dma((heads,)),
            dma((heads,)),
            dma((heads, n)),
            dma((heads, n)),
            dma((ns,)),
            dma((ns,)),
        ],
        compiler_params=pltpu.CompilerParams(
            collective_id=0, has_side_effects=True, vmem_limit_bytes=48 * 1024 * 1024
        ),
        cost_estimate=pl.CostEstimate(
            flops=2_000_000_000, bytes_accessed=5_000_000, transcendentals=1_600_000
        ),
    )(*args)
    return pl.pallas_call(
        store_kernel,
        out_shape=out_shape,
        in_specs=[vmem] * 5,
        out_specs=(hbm,) * 5,
        scratch_shapes=[dma((5,))],
        compiler_params=pltpu.CompilerParams(vmem_limit_bytes=4 * 1024 * 1024),
    )(*(pltpu.with_memory_space_constraint(array, pltpu.VMEM) for array in results))


def solution(mesh):
    rows = P(("sample", "prefix"), None, None)
    prompt = P("prefix", None)
    return jax.shard_map(
        body,
        mesh=mesh,
        in_specs=(rows, rows, rows, rows, rows, rows, prompt, prompt, P(("sample", "prefix"))),
        out_specs=(rows, rows, rows, prompt, prompt),
        check_vma=False,
    )
```

```python
import functools
import math

import jax
import jax.numpy as jnp
from jax import lax
from jax.experimental import pallas as pl
from jax.experimental.pallas import tpu as pltpu
from jax.sharding import PartitionSpec as P

H = 32
KVH = 4
HD = 128
G = H // KVH
MESH = pl.DeviceIdType.MESH
NT = (((1,), (1,)), ((), ()))
LOG2E = math.log2(math.e)
SCALE = HD ** (-0.5)
UB = 256


def dot(a, b):
    return jnp.dot(a, b, preferred_element_type=jnp.float32)


def dot_nt(a, b):
    return lax.dot_general(a, b, NT, preferred_element_type=jnp.float32)


def head_pair(ref, j):
    def read(first):
        at = [pl.ds(pl.multiple_of((j * G + g) * HD, HD), HD) for g in (first, first + 1)]
        return jnp.concatenate([ref[:, cols] for cols in at], 0)

    return read


def rows_to_lanes(block):
    return jnp.concatenate([block[g : g + 1] for g in range(G)], 1)


def part_grads(keys, values, queries, grads, lse_row, delta_row, live, keep):
    tokens = lse_row.shape[1] // G
    dk = dv = None

    def products(first):
        query, grad = queries(first), grads(first)
        return query, grad, dot_nt(keys, query), dot_nt(values, grad)

    ahead = products(0)
    for first in range(0, G, 2):
        query, grad, scores, prob_grad = ahead
        if first + 2 < G:
            ahead = products(first + 2)
        chunk = slice(first * tokens, (first + 2) * tokens)
        probs = jnp.exp2(scores * (SCALE * LOG2E) - lse_row[:, chunk])
        if live is not None:
            probs = jnp.where(live, probs, 0.0)
        dv_term = dot(probs.astype(jnp.bfloat16), grad)
        score_low = (probs * (prob_grad - delta_row[:, chunk])).astype(jnp.bfloat16)
        keep(chunk, score_low)
        dk_term = dot(score_low, query)
        dk = dk_term if dk is None else dk + dk_term
        dv = dv_term if dv is None else dv + dv_term
    return dk * SCALE, dv


def kernel(
    n, ns, rows, length_hbm, q_hbm, k_hbm, v_hbm, do_hbm, out_hbm, lse_hbm, pk_hbm, pv_hbm,
    dq_hbm, dk_hbm, dv_hbm, pdk_ref, pdv_ref,
    dk_ref, dv_ref, length_ref, q_ref, k_ref, v_ref, do_ref, out_ref, lse_ref, dq_ref, lse_t, delta_t, score_grads,
    gathered, crossed, parts, landed, totals,
    load_sem, store_sem, gather_send, gather_recv, pass_send, pass_recv, cross_send, cross_recv,
    part_send, part_recv, total_send, total_recv,
):
    tokens = q_ref.shape[0]
    me = lax.axis_index("prefix")
    mine = lax.axis_index("sample")
    half = lax.rem(mine, 2)
    partner = {"sample": mine + 1 - 2 * half}
    heads = KVH // 2
    width = KVH * HD

    pairs = [
        (pk_hbm, gathered.at[0, 0]), (pv_hbm, gathered.at[1, 0]),
        (do_hbm.at[0], do_ref), (out_hbm.at[0], out_ref),
        (lse_hbm.at[0], lse_ref), (q_hbm.at[0], q_ref), (k_hbm.at[0], k_ref), (v_hbm.at[0], v_ref),
        (length_hbm, length_ref),
    ]
    loads = [pltpu.make_async_copy(a, b, load_sem.at[i]) for i, (a, b) in enumerate(pairs)]

    barrier = pltpu.get_barrier_semaphore()

    def greet(d, _):
        pl.semaphore_signal(
            barrier, inc=1, device_id={"prefix": lax.rem(me + d, n)}, device_id_type=MESH
        )
        return 0

    def greet_sample(d, _):
        pl.semaphore_signal(
            barrier, inc=1, device_id={"sample": lax.rem(mine + d, ns)}, device_id_type=MESH
        )
        return 0

    lax.fori_loop(1, n, greet, 0)
    lax.fori_loop(1, ns, greet_sample, 0)
    for copy in loads:
        copy.start()
    pl.semaphore_wait(barrier, n - 1 + ns - 1)

    def gather_copy(d, source=pk_hbm):
        return pltpu.make_async_remote_copy(
            src_ref=source,
            dst_ref=gathered.at[half, d],
            send_sem=gather_send.at[d],
            recv_sem=gather_recv.at[d],
            device_id={"prefix": lax.rem(me + d, n)},
            device_id_type=MESH,
        )

    for which, source in enumerate((pk_hbm, pv_hbm)):

        @pl.when(half == which)
        def _():
            def start_gather(d, _):
                gather_copy(d, source).start()
                return 0

            lax.fori_loop(1, n, start_gather, 0)

    for copy in loads:
        copy.wait()
    length = length_ref[0]
    key_pos = lax.broadcasted_iota(jnp.int32, (tokens, tokens), 0)
    query_pos = lax.broadcasted_iota(jnp.int32, (tokens, tokens), 1)
    causal = key_pos <= query_pos
    live_t = lax.broadcasted_iota(jnp.int32, (H, tokens), 1) < length
    lse_t[...] = jnp.where(live_t, lse_ref[...] * LOG2E, 1e30)
    lanes = lax.broadcasted_iota(jnp.int32, (tokens, HD), 1)
    deltas = jnp.zeros((tokens, HD), jnp.float32)
    for h in range(H):
        at = slice(h * HD, (h + 1) * HD)
        product = do_ref[:, at].astype(jnp.float32) * out_ref[:, at].astype(jnp.float32)
        deltas = jnp.where(lanes == h, jnp.sum(product, 1, keepdims=True), deltas)
    delta_t[...] = deltas.T
    prompt_rows = n * rows

    def own_step(j, _):
        head = pl.ds(pl.multiple_of(j * HD, HD), HD)
        stat = pl.ds(pl.multiple_of(j * G, G), G)
        delta_row = rows_to_lanes(delta_t[stat, :])
        lse_row = rows_to_lanes(lse_t[stat, :])

        def keep(chunk, score_low):
            score_grads[j, prompt_rows:, chunk] = score_low

        dk, dv = part_grads(
            k_ref[:, head], v_ref[:, head], head_pair(q_ref, j), head_pair(do_ref, j),
            lse_row, delta_row, jnp.concatenate([causal] * 2, 1), keep,
        )
        dk_ref[:, head] = dk.astype(jnp.bfloat16)
        dv_ref[:, head] = dv.astype(jnp.bfloat16)
        return 0

    lax.fori_loop(0, KVH, own_step, 0)
    stores = [
        pltpu.make_async_copy(dk_ref, dk_hbm.at[0], store_sem.at[0]),
        pltpu.make_async_copy(dv_ref, dv_hbm.at[0], store_sem.at[1]),
        pltpu.make_async_copy(dq_ref, dq_hbm.at[0], store_sem.at[2]),
    ]
    stores[0].start()
    stores[1].start()

    def pass_copy(d):
        return pltpu.make_async_remote_copy(
            src_ref=gathered.at[half, d],
            dst_ref=gathered.at[half, d],
            send_sem=pass_send.at[d],
            recv_sem=pass_recv.at[d],
            device_id=partner,
            device_id_type=MESH,
        )

    def pass_on(d, _):
        gather_copy(d).wait_recv()
        pass_copy(d).start()
        return 0

    def end_pass(d, _):
        pass_copy(d).wait_recv()
        return 0

    lax.fori_loop(1, n, pass_on, 0)
    lax.fori_loop(1, n, end_pass, 0)

    block = UB if prompt_rows % UB == 0 else prompt_rows

    def prompt_head(j, use):
        head = pl.ds(pl.multiple_of(j * HD, HD), HD)
        stat = pl.ds(pl.multiple_of(j * G, G), G)
        lse_row = rows_to_lanes(lse_t[stat, :])
        delta_row = rows_to_lanes(delta_t[stat, :])

        def block_step(b, _):
            at = pl.ds(pl.multiple_of(b * block, block), block)
            slots = pl.ds(b * (block // rows), block // rows)

            def keep(chunk, score_low):
                score_grads[j, at, chunk] = score_low

            dk, dv = part_grads(
                gathered[0, slots, :, head].reshape(block, HD),
                gathered[1, slots, :, head].reshape(block, HD),
                head_pair(q_ref, j), head_pair(do_ref, j), lse_row, delta_row, None, keep,
            )
            use(slots, jnp.concatenate([dk, dv], 1).reshape(block // rows, rows, 2 * HD))
            return 0

        if prompt_rows == block:
            block_step(0, 0)
        else:
            lax.fori_loop(0, prompt_rows // block, block_step, 0)

    def cross_copy(i):
        return pltpu.make_async_remote_copy(
            src_ref=crossed.at[0, i],
            dst_ref=crossed.at[1, i],
            send_sem=cross_send.at[i],
            recv_sem=cross_recv.at[i],
            device_id=partner,
            device_id_type=MESH,
        )

    def cross_step(i, _):
        def use(slots, both):
            crossed[0, i, slots] = both

        prompt_head((1 - half) * heads + i, use)
        cross_copy(i).start()
        return 0

    for i in range(heads):
        cross_step(i, 0)

    def part_copy(i, d):
        return pltpu.make_async_remote_copy(
            src_ref=parts.at[i, d],
            dst_ref=landed.at[i, d],
            send_sem=part_send.at[i, d],
            recv_sem=part_recv.at[i, d],
            device_id={"prefix": lax.rem(me + n - d, n)},
            device_id_type=MESH,
        )

    def part_step(i, _):
        cross_copy(i).wait_recv()

        def use(slots, both):
            parts[i, slots] = (both + crossed[1, i, slots]).astype(jnp.bfloat16)

        prompt_head(half * heads + i, use)

        def start_part(d, _):
            part_copy(i, d).start()
            return 0

        lax.fori_loop(1, n, start_part, 0)
        return 0

    for i in range(heads):
        part_step(i, 0)

    def query_step(j, _):
        head = pl.ds(pl.multiple_of(j * HD, HD), HD)
        keys = jnp.concatenate(
            [gathered[0, :, :, head].reshape(prompt_rows, HD), k_ref[:, head]], 0
        )
        dq_t = (dot(keys.T, score_grads[j]) * SCALE).astype(jnp.bfloat16)
        for g in range(G):
            at = pl.ds(pl.multiple_of((j * G + g) * HD, HD), HD)
            dq_ref[:, at] = dq_t[:, g * HD : (g + 1) * HD].T
        return 0

    lax.fori_loop(0, KVH, query_step, 0)
    stores[2].start()

    def end_sends(d, _):
        gather_copy(d).wait_send()
        pass_copy(d).wait_send()
        return 0

    lax.fori_loop(1, n, end_sends, 0)
    for i in range(heads):
        cross_copy(i).wait_send()

    def sum_step(i, _):
        def wait_part(d, _):
            part_copy(i, d).wait()
            return 0

        lax.fori_loop(1, n, wait_part, 0)
        others = jnp.sum(landed[i, 1:].astype(jnp.float32), 0)
        totals[mine, i] = others + parts[i, 0].astype(jnp.float32)
        return 0

    lax.fori_loop(0, heads, sum_step, 0)

    def total_copy(d):
        return pltpu.make_async_remote_copy(
            src_ref=totals.at[mine],
            dst_ref=totals.at[mine],
            send_sem=total_send.at[d],
            recv_sem=total_recv.at[d],
            device_id={"sample": lax.rem(mine + d, ns)},
            device_id_type=MESH,
        )

    for d in range(1, ns):
        total_copy(d).start()
    for d in range(1, ns):
        total_copy(d).wait()
    for j in range(KVH):
        both = totals[j // heads, j % heads]
        for s in range(2 + j // heads, ns, 2):
            both = both + totals[s, j % heads]
        pdk_ref[:, j * HD : (j + 1) * HD] = both[:, :HD]
        pdv_ref[:, j * HD : (j + 1) * HD] = both[:, HD:]
    for store in stores:
        store.wait()


def store_kernel(*refs):
    *arrays, sem = refs
    count = len(arrays) // 2
    copies = [
        pltpu.make_async_copy(arrays[i], arrays[count + i], sem.at[i]) for i in range(count)
    ]
    for copy in copies:
        copy.start()
    for copy in copies:
        copy.wait()


def body(resp_q, resp_k, resp_v, resp_do, resp_out, resp_lse, prompt_k, prompt_v, resp_lengths):
    n = lax.axis_size("prefix")
    ns = lax.axis_size("sample")
    rows, width = prompt_k.shape
    _, tokens, q_width = resp_q.shape
    bf16, f32 = jnp.bfloat16, jnp.float32
    heads = KVH // 2
    vmem = pl.BlockSpec(memory_space=pltpu.VMEM)
    hbm = pl.BlockSpec(memory_space=pltpu.HBM)
    free = pl.BlockSpec(memory_space=pl.ANY)
    dma = pltpu.SemaphoreType.DMA
    out_shape = (
        jax.ShapeDtypeStruct(resp_q.shape, bf16),
        jax.ShapeDtypeStruct(resp_k.shape, bf16),
        jax.ShapeDtypeStruct(resp_v.shape, bf16),
        jax.ShapeDtypeStruct((rows, width), f32),
        jax.ShapeDtypeStruct((rows, width), f32),
    )
    args = (
        resp_lengths, resp_q, resp_k, resp_v, resp_do, resp_out, jnp.swapaxes(resp_lse, 1, 2),
        prompt_k, prompt_v,
    )
    args = args[:1] + tuple(pltpu.with_memory_space_constraint(arg, pltpu.HBM) for arg in args[1:])
    results = pl.pallas_call(
        functools.partial(kernel, n, ns, rows),
        out_shape=tuple(pltpu.VMEM(o.shape, o.dtype) for o in out_shape),
        in_specs=[hbm] * 9,
        out_specs=(free, free, free, vmem, vmem),
        scratch_shapes=[
            pltpu.VMEM((tokens, width), bf16),
            pltpu.VMEM((tokens, width), bf16),
            pltpu.SMEM((1,), jnp.int32),
            pltpu.VMEM((tokens, q_width), bf16),
            pltpu.VMEM((tokens, width), bf16),
            pltpu.VMEM((tokens, width), bf16),
            pltpu.VMEM((tokens, q_width), bf16),
            pltpu.VMEM((tokens, q_width), bf16),
            pltpu.VMEM((H, tokens), f32),
            pltpu.VMEM((tokens, q_width), bf16),
            pltpu.VMEM((H, tokens), f32),
            pltpu.VMEM((HD, tokens), f32),
            pltpu.VMEM((KVH, n * rows + tokens, G * tokens), bf16),
            pltpu.VMEM((2, n, rows, width), bf16),
            pltpu.VMEM((2, heads, n, rows, 2 * HD), f32),
            pltpu.VMEM((heads, n, rows, 2 * HD), bf16),
            pltpu.VMEM((heads, n, rows, 2 * HD), bf16),
            pltpu.VMEM((ns, heads, rows, 2 * HD), f32),
            dma((9,)),
            dma((3,)),
            dma((n,)),
            dma((n,)),
            dma((n,)),
            dma((n,)),
            dma((heads,)),
            dma((heads,)),
            dma((heads, n)),
            dma((heads, n)),
            dma((ns,)),
            dma((ns,)),
        ],
        compiler_params=pltpu.CompilerParams(
            collective_id=0, has_side_effects=True, vmem_limit_bytes=48 * 1024 * 1024
        ),
        cost_estimate=pl.CostEstimate(
            flops=2_000_000_000, bytes_accessed=5_000_000, transcendentals=1_600_000
        ),
    )(*args)
    return pl.pallas_call(
        store_kernel,
        out_shape=out_shape,
        in_specs=[vmem] * 5,
        out_specs=(hbm,) * 5,
        scratch_shapes=[dma((5,))],
        compiler_params=pltpu.CompilerParams(vmem_limit_bytes=4 * 1024 * 1024),
    )(*(pltpu.with_memory_space_constraint(array, pltpu.VMEM) for array in results))


def solution(mesh):
    rows = P(("sample", "prefix"), None, None)
    prompt = P("prefix", None)
    return jax.shard_map(
        body,
        mesh=mesh,
        in_specs=(rows, rows, rows, rows, rows, rows, prompt, prompt, P(("sample", "prefix"))),
        out_specs=(rows, rows, rows, prompt, prompt),
        check_vma=False,
    )
```

```python
import functools
import math

import jax
import jax.numpy as jnp
from jax import lax
from jax.experimental import pallas as pl
from jax.experimental.pallas import tpu as pltpu
from jax.sharding import PartitionSpec as P

H = 32
KVH = 4
HD = 128
G = H // KVH
MESH = pl.DeviceIdType.MESH
NT = (((1,), (1,)), ((), ()))
LOG2E = math.log2(math.e)
SCALE = HD ** (-0.5)
UB = 256


def dot(a, b):
    return jnp.dot(a, b, preferred_element_type=jnp.float32)


def dot_nt(a, b):
    return lax.dot_general(a, b, NT, preferred_element_type=jnp.float32)


def head_pair(ref, j):
    def read(first):
        at = [pl.ds(pl.multiple_of((j * G + g) * HD, HD), HD) for g in (first, first + 1)]
        return jnp.concatenate([ref[:, cols] for cols in at], 0)

    return read


def rows_to_lanes(block):
    return jnp.concatenate([block[g : g + 1] for g in range(G)], 1)


def part_grads(keys, values, queries, grads, lse_row, delta_row, live, keep):
    tokens = lse_row.shape[1] // G
    dk = dv = None

    def products(first):
        query, grad = queries(first), grads(first)
        return query, grad, dot_nt(keys, query), dot_nt(values, grad)

    ahead = products(0)
    for first in range(0, G, 2):
        query, grad, scores, prob_grad = ahead
        if first + 2 < G:
            ahead = products(first + 2)
        chunk = slice(first * tokens, (first + 2) * tokens)
        probs = jnp.exp2(scores * (SCALE * LOG2E) - lse_row[:, chunk])
        if live is not None:
            probs = jnp.where(live, probs, 0.0)
        dv_term = dot(probs.astype(jnp.bfloat16), grad)
        score_low = (probs * (prob_grad - delta_row[:, chunk])).astype(jnp.bfloat16)
        keep(chunk, score_low)
        dk_term = dot(score_low, query)
        dk = dk_term if dk is None else dk + dk_term
        dv = dv_term if dv is None else dv + dv_term
    return dk * SCALE, dv


def kernel(
    n, ns, rows, length_hbm, q_hbm, k_hbm, v_hbm, do_hbm, out_hbm, lse_hbm, pk_hbm, pv_hbm,
    dq_hbm, dk_hbm, dv_hbm, pdk_ref, pdv_ref,
    dk_ref, dv_ref, length_ref, q_ref, k_ref, v_ref, do_ref, out_ref, lse_ref, dq_ref,
    stats, own_low, prompt_low, q_other, do_other, stats_other, dq_other,
    gathered, parts, landed, totals,
    load_sem, store_sem, gather_send, gather_recv, swap_send, swap_recv, back_send, back_recv,
    part_send, part_recv, total_send, total_recv,
):
    tokens = q_ref.shape[0]
    me = lax.axis_index("prefix")
    mine = lax.axis_index("sample")
    half = lax.rem(mine, 2)
    partner = {"sample": mine + 1 - 2 * half}
    heads = KVH // 2
    prompt_rows = n * rows

    def half_cols(which, size):
        return pl.ds(pl.multiple_of(which * size, size), size)

    prompt_cols = half_cols(half, heads * HD)
    pairs = [
        (pk_hbm.at[:, prompt_cols], gathered.at[0, 0]),
        (pv_hbm.at[:, prompt_cols], gathered.at[0, 1]),
        (do_hbm.at[0], do_ref), (out_hbm.at[0], out_ref),
        (lse_hbm.at[0], lse_ref), (q_hbm.at[0], q_ref), (k_hbm.at[0], k_ref), (v_hbm.at[0], v_ref),
        (length_hbm, length_ref),
    ]
    loads = [pltpu.make_async_copy(a, b, load_sem.at[i]) for i, (a, b) in enumerate(pairs)]
    loads[0].start()
    loads[1].start()

    barrier = pltpu.get_barrier_semaphore()

    def greet(d, _):
        pl.semaphore_signal(
            barrier, inc=1, device_id={"prefix": lax.rem(me + d, n)}, device_id_type=MESH
        )
        return 0

    def greet_sample(d, _):
        pl.semaphore_signal(
            barrier, inc=1, device_id={"sample": lax.rem(mine + d, ns)}, device_id_type=MESH
        )
        return 0

    lax.fori_loop(1, n, greet, 0)
    lax.fori_loop(1, ns, greet_sample, 0)
    for copy in loads[2:]:
        copy.start()
    loads[0].wait()
    loads[1].wait()
    pl.semaphore_wait(barrier, n - 1 + ns - 1)

    def gather_copy(d):
        return pltpu.make_async_remote_copy(
            src_ref=gathered.at[0],
            dst_ref=gathered.at[d],
            send_sem=gather_send.at[d],
            recv_sem=gather_recv.at[d],
            device_id={"prefix": lax.rem(me + d, n)},
            device_id_type=MESH,
        )

    def start_gather(d, _):
        gather_copy(d).start()
        return 0

    lax.fori_loop(1, n, start_gather, 0)

    def swap_copy(i, source, target):
        return pltpu.make_async_remote_copy(
            src_ref=source,
            dst_ref=target,
            send_sem=swap_send.at[i],
            recv_sem=swap_recv.at[i],
            device_id=partner,
            device_id_type=MESH,
        )

    query_cols = half_cols(1 - half, heads * G * HD)
    swaps = [
        swap_copy(0, q_hbm.at[0, :, query_cols], q_other),
        swap_copy(1, do_hbm.at[0, :, query_cols], do_other),
        swap_copy(2, stats.at[:, half_cols(1 - half, heads * G)], stats_other),
    ]
    swaps[0].start()
    swaps[1].start()
    for copy in loads[2:]:
        copy.wait()
    length = length_ref[0]
    key_pos = lax.broadcasted_iota(jnp.int32, (tokens, tokens), 0)
    query_pos = lax.broadcasted_iota(jnp.int32, (tokens, tokens), 1)
    causal = key_pos <= query_pos
    live_t = lax.broadcasted_iota(jnp.int32, (H, tokens), 1) < length
    stats[0] = jnp.where(live_t, lse_ref[...] * LOG2E, 1e30)
    lanes = lax.broadcasted_iota(jnp.int32, (tokens, HD), 1)
    deltas = jnp.zeros((tokens, HD), jnp.float32)
    for h in range(H):
        at = slice(h * HD, (h + 1) * HD)
        product = do_ref[:, at].astype(jnp.float32) * out_ref[:, at].astype(jnp.float32)
        deltas = jnp.where(lanes == h, jnp.sum(product, 1, keepdims=True), deltas)
    stats[1] = deltas.T[:H]
    swaps[2].start()

    def own_step(j, _):
        head = pl.ds(pl.multiple_of(j * HD, HD), HD)
        stat = pl.ds(pl.multiple_of(j * G, G), G)
        lse_row = rows_to_lanes(stats[0, stat, :])
        delta_row = rows_to_lanes(stats[1, stat, :])

        def keep(chunk, score_low):
            own_low[j, :, chunk] = score_low

        dk, dv = part_grads(
            k_ref[:, head], v_ref[:, head], head_pair(q_ref, j), head_pair(do_ref, j),
            lse_row, delta_row, jnp.concatenate([causal] * 2, 1), keep,
        )
        dk_ref[:, head] = dk.astype(jnp.bfloat16)
        dv_ref[:, head] = dv.astype(jnp.bfloat16)
        return 0

    lax.fori_loop(0, KVH, own_step, 0)
    stores = [
        pltpu.make_async_copy(dk_ref, dk_hbm.at[0], store_sem.at[0]),
        pltpu.make_async_copy(dv_ref, dv_hbm.at[0], store_sem.at[1]),
        pltpu.make_async_copy(dq_ref, dq_hbm.at[0], store_sem.at[2]),
    ]
    stores[0].start()
    stores[1].start()

    def end_gather(d, _):
        gather_copy(d).wait()
        return 0

    lax.fori_loop(1, n, end_gather, 0)
    for copy in swaps:
        copy.wait()

    block = UB if prompt_rows % UB == 0 else prompt_rows

    def part_copy(i, d):
        return pltpu.make_async_remote_copy(
            src_ref=parts.at[i, d],
            dst_ref=landed.at[i, d],
            send_sem=part_send.at[i, d],
            recv_sem=part_recv.at[i, d],
            device_id={"prefix": lax.rem(me + n - d, n)},
            device_id_type=MESH,
        )

    def part_step(i):
        head = slice(i * HD, (i + 1) * HD)
        j = half * heads + i
        own_stat = pl.ds(pl.multiple_of(j * G, G), G)
        other_stat = slice(i * G, (i + 1) * G)
        sides = (
            (head_pair(q_ref, j), head_pair(do_ref, j), stats[0, own_stat], stats[1, own_stat]),
            (
                head_pair(q_other, i), head_pair(do_other, i),
                stats_other[0, other_stat], stats_other[1, other_stat],
            ),
        )

        def block_step(b, _):
            at = pl.ds(pl.multiple_of(b * block, block), block)
            slots = pl.ds(b * (block // rows), block // rows)
            keys = gathered[slots, 0, :, head].reshape(block, HD)
            values = gathered[slots, 1, :, head].reshape(block, HD)
            both = None
            for side, (queries, grads, lse, delta) in enumerate(sides):

                def keep(chunk, score_low):
                    prompt_low[side, i, at, chunk] = score_low

                dk, dv = part_grads(
                    keys, values, queries, grads, rows_to_lanes(lse), rows_to_lanes(delta), None,
                    keep,
                )
                term = jnp.concatenate([dk, dv], 1)
                both = term if both is None else both + term
            parts[i, slots] = both.astype(jnp.bfloat16).reshape(block // rows, rows, 2 * HD)
            return 0

        if prompt_rows == block:
            block_step(0, 0)
        else:
            lax.fori_loop(0, prompt_rows // block, block_step, 0)

        def start_part(d, _):
            part_copy(i, d).start()
            return 0

        lax.fori_loop(1, n, start_part, 0)

    for i in range(heads):
        part_step(i)

    def back_copy(i):
        return pltpu.make_async_remote_copy(
            src_ref=dq_other.at[0, i],
            dst_ref=dq_other.at[1, i],
            send_sem=back_send.at[i],
            recv_sem=back_recv.at[i],
            device_id=partner,
            device_id_type=MESH,
        )

    def prompt_term(side, i):
        keys = gathered[:, 0, :, i * HD : (i + 1) * HD].reshape(prompt_rows, HD)
        return dot(keys.T, prompt_low[side, i])

    def store_queries(j, prompt_sum):
        keys = k_ref[:, pl.ds(pl.multiple_of(j * HD, HD), HD)]
        dq_t = ((prompt_sum + dot(keys.T, own_low[j])) * SCALE).astype(jnp.bfloat16)
        for g in range(G):
            at = pl.ds(pl.multiple_of((j * G + g) * HD, HD), HD)
            dq_ref[:, at] = dq_t[:, g * HD : (g + 1) * HD].T

    for i in range(heads):
        dq_other[0, i] = prompt_term(1, i)
        back_copy(i).start()
    for i in range(heads):
        store_queries(half * heads + i, prompt_term(0, i))
    for i in range(heads):
        back_copy(i).wait()
        store_queries((1 - half) * heads + i, dq_other[1, i])
    stores[2].start()

    def sum_step(i, _):
        def wait_part(d, _):
            part_copy(i, d).wait()
            return 0

        lax.fori_loop(1, n, wait_part, 0)
        others = jnp.sum(landed[i, 1:].astype(jnp.float32), 0)
        totals[mine, i] = others + parts[i, 0].astype(jnp.float32)
        return 0

    lax.fori_loop(0, heads, sum_step, 0)

    def total_copy(d):
        return pltpu.make_async_remote_copy(
            src_ref=totals.at[mine],
            dst_ref=totals.at[mine],
            send_sem=total_send.at[d],
            recv_sem=total_recv.at[d],
            device_id={"sample": lax.rem(mine + d, ns)},
            device_id_type=MESH,
        )

    for d in range(1, ns):
        total_copy(d).start()
    for d in range(1, ns):
        total_copy(d).wait()
    for j in range(KVH):
        both = totals[j // heads, j % heads]
        for s in range(2 + j // heads, ns, 2):
            both = both + totals[s, j % heads]
        pdk_ref[:, j * HD : (j + 1) * HD] = both[:, :HD]
        pdv_ref[:, j * HD : (j + 1) * HD] = both[:, HD:]
    for store in stores:
        store.wait()


def store_kernel(*refs):
    *arrays, sem = refs
    count = len(arrays) // 2
    copies = [
        pltpu.make_async_copy(arrays[i], arrays[count + i], sem.at[i]) for i in range(count)
    ]
    for copy in copies:
        copy.start()
    for copy in copies:
        copy.wait()


def body(resp_q, resp_k, resp_v, resp_do, resp_out, resp_lse, prompt_k, prompt_v, resp_lengths):
    n = lax.axis_size("prefix")
    ns = lax.axis_size("sample")
    rows, width = prompt_k.shape
    _, tokens, q_width = resp_q.shape
    bf16, f32 = jnp.bfloat16, jnp.float32
    heads = KVH // 2
    vmem = pl.BlockSpec(memory_space=pltpu.VMEM)
    hbm = pl.BlockSpec(memory_space=pltpu.HBM)
    free = pl.BlockSpec(memory_space=pl.ANY)
    dma = pltpu.SemaphoreType.DMA
    out_shape = (
        jax.ShapeDtypeStruct(resp_q.shape, bf16),
        jax.ShapeDtypeStruct(resp_k.shape, bf16),
        jax.ShapeDtypeStruct(resp_v.shape, bf16),
        jax.ShapeDtypeStruct((rows, width), f32),
        jax.ShapeDtypeStruct((rows, width), f32),
    )
    args = (
        resp_lengths, resp_q, resp_k, resp_v, resp_do, resp_out, jnp.swapaxes(resp_lse, 1, 2),
        prompt_k, prompt_v,
    )
    args = args[:1] + tuple(pltpu.with_memory_space_constraint(arg, pltpu.HBM) for arg in args[1:])
    results = pl.pallas_call(
        functools.partial(kernel, n, ns, rows),
        out_shape=tuple(pltpu.VMEM(o.shape, o.dtype) for o in out_shape),
        in_specs=[hbm] * 9,
        out_specs=(free, free, free, vmem, vmem),
        scratch_shapes=[
            pltpu.VMEM((tokens, width), bf16),
            pltpu.VMEM((tokens, width), bf16),
            pltpu.SMEM((1,), jnp.int32),
            pltpu.VMEM((tokens, q_width), bf16),
            pltpu.VMEM((tokens, width), bf16),
            pltpu.VMEM((tokens, width), bf16),
            pltpu.VMEM((tokens, q_width), bf16),
            pltpu.VMEM((tokens, q_width), bf16),
            pltpu.VMEM((H, tokens), f32),
            pltpu.VMEM((tokens, q_width), bf16),
            pltpu.VMEM((2, H, tokens), f32),
            pltpu.VMEM((KVH, tokens, G * tokens), bf16),
            pltpu.VMEM((2, heads, n * rows, G * tokens), bf16),
            pltpu.VMEM((tokens, q_width // 2), bf16),
            pltpu.VMEM((tokens, q_width // 2), bf16),
            pltpu.VMEM((2, H // 2, tokens), f32),
            pltpu.VMEM((2, heads, HD, G * tokens), f32),
            pltpu.VMEM((n, 2, rows, heads * HD), bf16),
            pltpu.VMEM((heads, n, rows, 2 * HD), bf16),
            pltpu.VMEM((heads, n, rows, 2 * HD), bf16),
            pltpu.VMEM((ns, heads, rows, 2 * HD), f32),
            dma((9,)),
            dma((3,)),
            dma((n,)),
            dma((n,)),
            dma((3,)),
            dma((3,)),
            dma((heads,)),
            dma((heads,)),
            dma((heads, n)),
            dma((heads, n)),
            dma((ns,)),
            dma((ns,)),
        ],
        compiler_params=pltpu.CompilerParams(
            collective_id=0, has_side_effects=True, vmem_limit_bytes=48 * 1024 * 1024
        ),
        cost_estimate=pl.CostEstimate(
            flops=2_000_000_000, bytes_accessed=5_000_000, transcendentals=1_600_000
        ),
    )(*args)
    return pl.pallas_call(
        store_kernel,
        out_shape=out_shape,
        in_specs=[vmem] * 5,
        out_specs=(hbm,) * 5,
        scratch_shapes=[dma((5,))],
        compiler_params=pltpu.CompilerParams(vmem_limit_bytes=4 * 1024 * 1024),
    )(*(pltpu.with_memory_space_constraint(array, pltpu.VMEM) for array in results))


def solution(mesh):
    rows = P(("sample", "prefix"), None, None)
    prompt = P("prefix", None)
    return jax.shard_map(
        body,
        mesh=mesh,
        in_specs=(rows, rows, rows, rows, rows, rows, prompt, prompt, P(("sample", "prefix"))),
        out_specs=(rows, rows, rows, prompt, prompt),
        check_vma=False,
    )
```

```python
import functools
import math

import jax
import jax.numpy as jnp
from jax import lax
from jax.experimental import pallas as pl
from jax.experimental.pallas import tpu as pltpu
from jax.sharding import PartitionSpec as P

H = 32
KVH = 4
HD = 128
G = H // KVH
MESH = pl.DeviceIdType.MESH
NT = (((1,), (1,)), ((), ()))
LOG2E = math.log2(math.e)
SCALE = HD ** (-0.5)
UB = 256


def dot(a, b):
    return jnp.dot(a, b, preferred_element_type=jnp.float32)


def dot_nt(a, b):
    return lax.dot_general(a, b, NT, preferred_element_type=jnp.float32)


def head_pair(ref, j):
    def read(first):
        at = [pl.ds(pl.multiple_of((j * G + g) * HD, HD), HD) for g in (first, first + 1)]
        return jnp.concatenate([ref[:, cols] for cols in at], 0)

    return read


def rows_to_lanes(block):
    return jnp.concatenate([block[g : g + 1] for g in range(G)], 1)


def part_grads(keys, values, queries, grads, lse_row, delta_row, live, keep):
    tokens = lse_row.shape[1] // G
    dk = dv = None

    def products(first):
        query, grad = queries(first), grads(first)
        return query, grad, dot_nt(keys, query), dot_nt(values, grad)

    ahead = products(0)
    for first in range(0, G, 2):
        query, grad, scores, prob_grad = ahead
        if first + 2 < G:
            ahead = products(first + 2)
        chunk = slice(first * tokens, (first + 2) * tokens)
        probs = jnp.exp2(scores * (SCALE * LOG2E) - lse_row[:, chunk])
        if live is not None:
            probs = jnp.where(live, probs, 0.0)
        dv_term = dot(probs.astype(jnp.bfloat16), grad)
        score_low = (probs * (prob_grad - delta_row[:, chunk])).astype(jnp.bfloat16)
        keep(chunk, score_low)
        dk_term = dot(score_low, query)
        dk = dk_term if dk is None else dk + dk_term
        dv = dv_term if dv is None else dv + dv_term
    return dk * SCALE, dv


def kernel(
    n, ns, rows, length_hbm, q_hbm, k_hbm, v_hbm, do_hbm, out_hbm, lse_hbm, pk_hbm, pv_hbm,
    dq_ref, dk_ref, dv_ref, pdk_ref, pdv_ref,
    length_ref, q_ref, k_ref, v_ref, do_ref, out_ref, lse_ref,
    stats, own_low, prompt_low, q_other, do_other, stats_other, dq_other,
    gathered, parts, landed, totals,
    load_sem, gather_send, gather_recv, swap_send, swap_recv, back_send, back_recv,
    part_send, part_recv, total_send, total_recv,
):
    tokens = q_ref.shape[0]
    me = lax.axis_index("prefix")
    mine = lax.axis_index("sample")
    half = lax.rem(mine, 2)
    partner = {"sample": mine + 1 - 2 * half}
    heads = KVH // 2
    prompt_rows = n * rows

    def half_cols(which, size):
        return pl.ds(pl.multiple_of(which * size, size), size)

    prompt_cols = half_cols(half, heads * HD)
    pairs = [
        (pk_hbm.at[:, prompt_cols], gathered.at[0, 0]),
        (pv_hbm.at[:, prompt_cols], gathered.at[0, 1]),
        (do_hbm.at[0], do_ref), (out_hbm.at[0], out_ref),
        (lse_hbm.at[0], lse_ref), (q_hbm.at[0], q_ref), (k_hbm.at[0], k_ref), (v_hbm.at[0], v_ref),
        (length_hbm, length_ref),
    ]
    loads = [pltpu.make_async_copy(a, b, load_sem.at[i]) for i, (a, b) in enumerate(pairs)]
    loads[0].start()
    loads[1].start()

    barrier = pltpu.get_barrier_semaphore()

    def greet(d, _):
        pl.semaphore_signal(
            barrier, inc=1, device_id={"prefix": lax.rem(me + d, n)}, device_id_type=MESH
        )
        return 0

    def greet_sample(d, _):
        pl.semaphore_signal(
            barrier, inc=1, device_id={"sample": lax.rem(mine + d, ns)}, device_id_type=MESH
        )
        return 0

    lax.fori_loop(1, n, greet, 0)
    lax.fori_loop(1, ns, greet_sample, 0)
    for copy in loads[2:]:
        copy.start()
    loads[0].wait()
    loads[1].wait()
    pl.semaphore_wait(barrier, n - 1 + ns - 1)

    def gather_copy(d):
        return pltpu.make_async_remote_copy(
            src_ref=gathered.at[0],
            dst_ref=gathered.at[d],
            send_sem=gather_send.at[d],
            recv_sem=gather_recv.at[d],
            device_id={"prefix": lax.rem(me + d, n)},
            device_id_type=MESH,
        )

    def start_gather(d, _):
        gather_copy(d).start()
        return 0

    lax.fori_loop(1, n, start_gather, 0)

    def swap_copy(i, source, target):
        return pltpu.make_async_remote_copy(
            src_ref=source,
            dst_ref=target,
            send_sem=swap_send.at[i],
            recv_sem=swap_recv.at[i],
            device_id=partner,
            device_id_type=MESH,
        )

    query_cols = half_cols(1 - half, heads * G * HD)
    swaps = [
        swap_copy(0, q_hbm.at[0, :, query_cols], q_other),
        swap_copy(1, do_hbm.at[0, :, query_cols], do_other),
        swap_copy(2, stats.at[:, half_cols(1 - half, heads * G)], stats_other),
    ]
    swaps[0].start()
    swaps[1].start()
    for copy in loads[2:]:
        copy.wait()
    length = length_ref[0]
    key_pos = lax.broadcasted_iota(jnp.int32, (tokens, tokens), 0)
    query_pos = lax.broadcasted_iota(jnp.int32, (tokens, tokens), 1)
    causal = key_pos <= query_pos
    live_t = lax.broadcasted_iota(jnp.int32, (H, tokens), 1) < length
    stats[0] = jnp.where(live_t, lse_ref[...] * LOG2E, 1e30)
    lanes = lax.broadcasted_iota(jnp.int32, (tokens, HD), 1)
    deltas = jnp.zeros((tokens, HD), jnp.float32)
    for h in range(H):
        at = slice(h * HD, (h + 1) * HD)
        product = do_ref[:, at].astype(jnp.float32) * out_ref[:, at].astype(jnp.float32)
        deltas = jnp.where(lanes == h, jnp.sum(product, 1, keepdims=True), deltas)
    stats[1] = deltas.T[:H]
    swaps[2].start()

    def own_step(i, _):
        j = lax.rem(half * heads + i, KVH)
        head = pl.ds(pl.multiple_of(j * HD, HD), HD)
        stat = pl.ds(pl.multiple_of(j * G, G), G)
        lse_row = rows_to_lanes(stats[0, stat, :])
        delta_row = rows_to_lanes(stats[1, stat, :])

        def keep(chunk, score_low):
            own_low[j, :, chunk] = score_low

        dk, dv = part_grads(
            k_ref[:, head], v_ref[:, head], head_pair(q_ref, j), head_pair(do_ref, j),
            lse_row, delta_row, jnp.concatenate([causal] * 2, 1), keep,
        )
        dk_ref[0, :, head] = dk.astype(jnp.bfloat16)
        dv_ref[0, :, head] = dv.astype(jnp.bfloat16)
        return 0

    lax.fori_loop(0, KVH - 1, own_step, 0)

    def end_gather(d, _):
        gather_copy(d).wait()
        return 0

    lax.fori_loop(1, n, end_gather, 0)
    for copy in swaps:
        copy.wait()

    block = UB if prompt_rows % UB == 0 else prompt_rows

    def part_copy(i, d):
        return pltpu.make_async_remote_copy(
            src_ref=parts.at[i, d],
            dst_ref=landed.at[i, d],
            send_sem=part_send.at[i, d],
            recv_sem=part_recv.at[i, d],
            device_id={"prefix": lax.rem(me + n - d, n)},
            device_id_type=MESH,
        )

    def part_step(i):
        head = slice(i * HD, (i + 1) * HD)
        j = half * heads + i
        own_stat = pl.ds(pl.multiple_of(j * G, G), G)
        other_stat = slice(i * G, (i + 1) * G)
        sides = (
            (head_pair(q_ref, j), head_pair(do_ref, j), stats[0, own_stat], stats[1, own_stat]),
            (
                head_pair(q_other, i), head_pair(do_other, i),
                stats_other[0, other_stat], stats_other[1, other_stat],
            ),
        )

        def block_step(b, _):
            at = pl.ds(pl.multiple_of(b * block, block), block)
            slots = pl.ds(b * (block // rows), block // rows)
            keys = gathered[slots, 0, :, head].reshape(block, HD)
            values = gathered[slots, 1, :, head].reshape(block, HD)
            both = None
            for side, (queries, grads, lse, delta) in enumerate(sides):

                def keep(chunk, score_low):
                    prompt_low[side, i, at, chunk] = score_low

                dk, dv = part_grads(
                    keys, values, queries, grads, rows_to_lanes(lse), rows_to_lanes(delta), None,
                    keep,
                )
                term = jnp.concatenate([dk, dv], 1)
                both = term if both is None else both + term
            parts[i, slots] = both.astype(jnp.bfloat16).reshape(block // rows, rows, 2 * HD)
            return 0

        if prompt_rows == block:
            block_step(0, 0)
        else:
            lax.fori_loop(0, prompt_rows // block, block_step, 0)

        def start_part(d, _):
            part_copy(i, d).start()
            return 0

        lax.fori_loop(1, n, start_part, 0)

    for i in range(heads):
        part_step(i)

    def back_copy(i):
        return pltpu.make_async_remote_copy(
            src_ref=dq_other.at[0, i],
            dst_ref=dq_other.at[1, i],
            send_sem=back_send.at[i],
            recv_sem=back_recv.at[i],
            device_id=partner,
            device_id_type=MESH,
        )

    def prompt_term(side, i):
        keys = gathered[:, 0, :, i * HD : (i + 1) * HD].reshape(prompt_rows, HD)
        return dot(keys.T, prompt_low[side, i])

    def store_queries(j, prompt_sum):
        keys = k_ref[:, pl.ds(pl.multiple_of(j * HD, HD), HD)]
        dq_t = ((prompt_sum + dot(keys.T, own_low[j])) * SCALE).astype(jnp.bfloat16)
        for g in range(G):
            at = pl.ds(pl.multiple_of((j * G + g) * HD, HD), HD)
            dq_ref[0, :, at] = dq_t[:, g * HD : (g + 1) * HD].T

    for i in range(heads):
        dq_other[0, i] = prompt_term(1, i)
        back_copy(i).start()
    own_step(KVH - 1, 0)
    for i in range(heads):
        store_queries(half * heads + i, prompt_term(0, i))
    for i in range(heads):
        back_copy(i).wait()
        store_queries((1 - half) * heads + i, dq_other[1, i])
    def sum_step(i, _):
        def wait_part(d, _):
            part_copy(i, d).wait()
            return 0

        lax.fori_loop(1, n, wait_part, 0)
        others = jnp.sum(landed[i, 1:].astype(jnp.float32), 0)
        totals[mine, i] = others + parts[i, 0].astype(jnp.float32)
        return 0

    lax.fori_loop(0, heads, sum_step, 0)

    def total_copy(d):
        return pltpu.make_async_remote_copy(
            src_ref=totals.at[mine],
            dst_ref=totals.at[mine],
            send_sem=total_send.at[d],
            recv_sem=total_recv.at[d],
            device_id={"sample": lax.rem(mine + d, ns)},
            device_id_type=MESH,
        )

    for d in range(1, ns):
        total_copy(d).start()
    for d in range(1, ns):
        total_copy(d).wait()
    for j in range(KVH):
        both = totals[j // heads, j % heads]
        for s in range(2 + j // heads, ns, 2):
            both = both + totals[s, j % heads]
        pdk_ref[:, j * HD : (j + 1) * HD] = both[:, :HD]
        pdv_ref[:, j * HD : (j + 1) * HD] = both[:, HD:]


def store_kernel(*refs):
    *arrays, sem = refs
    count = len(arrays) // 2
    copies = [
        pltpu.make_async_copy(arrays[i], arrays[count + i], sem.at[i]) for i in range(count)
    ]
    for copy in copies:
        copy.start()
    for copy in copies:
        copy.wait()


def body(resp_q, resp_k, resp_v, resp_do, resp_out, resp_lse, prompt_k, prompt_v, resp_lengths):
    n = lax.axis_size("prefix")
    ns = lax.axis_size("sample")
    rows, width = prompt_k.shape
    _, tokens, q_width = resp_q.shape
    bf16, f32 = jnp.bfloat16, jnp.float32
    heads = KVH // 2
    vmem = pl.BlockSpec(memory_space=pltpu.VMEM)
    hbm = pl.BlockSpec(memory_space=pltpu.HBM)
    dma = pltpu.SemaphoreType.DMA
    out_shape = (
        jax.ShapeDtypeStruct(resp_q.shape, bf16),
        jax.ShapeDtypeStruct(resp_k.shape, bf16),
        jax.ShapeDtypeStruct(resp_v.shape, bf16),
        jax.ShapeDtypeStruct((rows, width), f32),
        jax.ShapeDtypeStruct((rows, width), f32),
    )
    args = (
        resp_lengths, resp_q, resp_k, resp_v, resp_do, resp_out, jnp.swapaxes(resp_lse, 1, 2),
        prompt_k, prompt_v,
    )
    args = args[:1] + tuple(pltpu.with_memory_space_constraint(arg, pltpu.HBM) for arg in args[1:])
    results = pl.pallas_call(
        functools.partial(kernel, n, ns, rows),
        out_shape=tuple(pltpu.VMEM(o.shape, o.dtype) for o in out_shape),
        in_specs=[hbm] * 9,
        out_specs=(vmem,) * 5,
        scratch_shapes=[
            pltpu.SMEM((1,), jnp.int32),
            pltpu.VMEM((tokens, q_width), bf16),
            pltpu.VMEM((tokens, width), bf16),
            pltpu.VMEM((tokens, width), bf16),
            pltpu.VMEM((tokens, q_width), bf16),
            pltpu.VMEM((tokens, q_width), bf16),
            pltpu.VMEM((H, tokens), f32),
            pltpu.VMEM((2, H, tokens), f32),
            pltpu.VMEM((KVH, tokens, G * tokens), bf16),
            pltpu.VMEM((2, heads, n * rows, G * tokens), bf16),
            pltpu.VMEM((tokens, q_width // 2), bf16),
            pltpu.VMEM((tokens, q_width // 2), bf16),
            pltpu.VMEM((2, H // 2, tokens), f32),
            pltpu.VMEM((2, heads, HD, G * tokens), f32),
            pltpu.VMEM((n, 2, rows, heads * HD), bf16),
            pltpu.VMEM((heads, n, rows, 2 * HD), bf16),
            pltpu.VMEM((heads, n, rows, 2 * HD), bf16),
            pltpu.VMEM((ns, heads, rows, 2 * HD), f32),
            dma((9,)),
            dma((n,)),
            dma((n,)),
            dma((3,)),
            dma((3,)),
            dma((heads,)),
            dma((heads,)),
            dma((heads, n)),
            dma((heads, n)),
            dma((ns,)),
            dma((ns,)),
        ],
        compiler_params=pltpu.CompilerParams(
            collective_id=0, has_side_effects=True, vmem_limit_bytes=48 * 1024 * 1024
        ),
        cost_estimate=pl.CostEstimate(
            flops=2_000_000_000, bytes_accessed=5_000_000, transcendentals=1_600_000
        ),
    )(*args)
    return pl.pallas_call(
        store_kernel,
        out_shape=out_shape,
        in_specs=[vmem] * 5,
        out_specs=(hbm,) * 5,
        scratch_shapes=[dma((5,))],
        compiler_params=pltpu.CompilerParams(vmem_limit_bytes=4 * 1024 * 1024),
    )(*(pltpu.with_memory_space_constraint(array, pltpu.VMEM) for array in results))


def solution(mesh):
    rows = P(("sample", "prefix"), None, None)
    prompt = P("prefix", None)
    return jax.shard_map(
        body,
        mesh=mesh,
        in_specs=(rows, rows, rows, rows, rows, rows, prompt, prompt, P(("sample", "prefix"))),
        out_specs=(rows, rows, rows, prompt, prompt),
        check_vma=False,
    )
```

```python
import functools
import math

import jax
import jax.numpy as jnp
from jax import lax
from jax.experimental import pallas as pl
from jax.experimental.pallas import tpu as pltpu
from jax.sharding import PartitionSpec as P

H = 32
KVH = 4
HD = 128
G = H // KVH
MESH = pl.DeviceIdType.MESH
NT = (((1,), (1,)), ((), ()))
LOG2E = math.log2(math.e)
SCALE = HD ** (-0.5)
UB = 256


def dot(a, b):
    return jnp.dot(a, b, preferred_element_type=jnp.float32)


def dot_nt(a, b):
    return lax.dot_general(a, b, NT, preferred_element_type=jnp.float32)


def head_pair(ref, j):
    def read(first):
        at = [pl.ds(pl.multiple_of((j * G + g) * HD, HD), HD) for g in (first, first + 1)]
        return jnp.concatenate([ref[:, cols] for cols in at], 0)

    return read


def rows_to_lanes(block):
    return jnp.concatenate([block[g : g + 1] for g in range(G)], 1)


def part_grads(keys, values, queries, grads, lse_row, delta_row, live, keep):
    tokens = lse_row.shape[1] // G
    dk = dv = None

    def products(first):
        query, grad = queries(first), grads(first)
        return query, grad, dot_nt(keys, query), dot_nt(values, grad)

    ahead = products(0)
    for first in range(0, G, 2):
        query, grad, scores, prob_grad = ahead
        if first + 2 < G:
            ahead = products(first + 2)
        chunk = slice(first * tokens, (first + 2) * tokens)
        probs = jnp.exp2(scores * (SCALE * LOG2E) - lse_row[:, chunk])
        if live is not None:
            probs = jnp.where(live, probs, 0.0)
        dv_term = dot(probs.astype(jnp.bfloat16), grad)
        score_low = (probs * (prob_grad - delta_row[:, chunk])).astype(jnp.bfloat16)
        keep(chunk, score_low)
        dk_term = dot(score_low, query)
        dk = dk_term if dk is None else dk + dk_term
        dv = dv_term if dv is None else dv + dv_term
    return dk * SCALE, dv


def kernel(
    n, ns, rows, length_hbm, q_hbm, k_hbm, v_hbm, do_hbm, out_hbm, lse_hbm, pk_hbm, pv_hbm,
    dq_ref, dk_ref, dv_ref, pdk_ref, pdv_ref,
    length_ref, q_ref, k_ref, v_ref, do_ref, out_ref, lse_ref,
    stats, own_low, prompt_low, q_other, do_other, stats_other, dq_other,
    gathered, parts, landed, totals,
    load_sem, gather_send, gather_recv, swap_send, swap_recv, back_send, back_recv,
    part_send, part_recv, total_send, total_recv,
):
    tokens = q_ref.shape[0]
    me = lax.axis_index("prefix")
    mine = lax.axis_index("sample")
    half = lax.rem(mine, 2)
    partner = {"sample": mine + 1 - 2 * half}
    heads = KVH // 2
    prompt_rows = n * rows

    def half_cols(which, size):
        return pl.ds(pl.multiple_of(which * size, size), size)

    prompt_cols = half_cols(half, heads * HD)
    pairs = [
        (pk_hbm.at[:, prompt_cols], gathered.at[0, 0]),
        (pv_hbm.at[:, prompt_cols], gathered.at[0, 1]),
        (do_hbm.at[0], do_ref), (out_hbm.at[0], out_ref),
        (lse_hbm.at[0], lse_ref), (q_hbm.at[0], q_ref), (k_hbm.at[0], k_ref), (v_hbm.at[0], v_ref),
        (length_hbm, length_ref),
    ]
    loads = [pltpu.make_async_copy(a, b, load_sem.at[i]) for i, (a, b) in enumerate(pairs)]
    loads[0].start()
    loads[1].start()

    barrier = pltpu.get_barrier_semaphore()

    def greet(d, _):
        pl.semaphore_signal(
            barrier, inc=1, device_id={"prefix": lax.rem(me + d, n)}, device_id_type=MESH
        )
        return 0

    def greet_sample(d, _):
        pl.semaphore_signal(
            barrier, inc=1, device_id={"sample": lax.rem(mine + d, ns)}, device_id_type=MESH
        )
        return 0

    lax.fori_loop(1, n, greet, 0)
    lax.fori_loop(1, ns, greet_sample, 0)
    for copy in loads[2:]:
        copy.start()
    loads[0].wait()
    loads[1].wait()
    pl.semaphore_wait(barrier, n - 1 + ns - 1)

    def gather_copy(d):
        return pltpu.make_async_remote_copy(
            src_ref=gathered.at[0],
            dst_ref=gathered.at[d],
            send_sem=gather_send.at[d],
            recv_sem=gather_recv.at[d],
            device_id={"prefix": lax.rem(me + d, n)},
            device_id_type=MESH,
        )

    def start_gather(d, _):
        gather_copy(d).start()
        return 0

    lax.fori_loop(1, n, start_gather, 0)

    def swap_copy(i, source, target):
        return pltpu.make_async_remote_copy(
            src_ref=source,
            dst_ref=target,
            send_sem=swap_send.at[i],
            recv_sem=swap_recv.at[i],
            device_id=partner,
            device_id_type=MESH,
        )

    query_cols = half_cols(1 - half, heads * G * HD)
    swaps = [
        swap_copy(0, q_hbm.at[0, :, query_cols], q_other),
        swap_copy(1, do_hbm.at[0, :, query_cols], do_other),
        swap_copy(2, stats.at[:, half_cols(1 - half, heads * G)], stats_other),
    ]
    swaps[0].start()
    swaps[1].start()
    for copy in loads[2:]:
        copy.wait()
    length = length_ref[0]
    key_pos = lax.broadcasted_iota(jnp.int32, (tokens, tokens), 0)
    query_pos = lax.broadcasted_iota(jnp.int32, (tokens, tokens), 1)
    causal = key_pos <= query_pos
    live_t = lax.broadcasted_iota(jnp.int32, (H, tokens), 1) < length
    stats[0] = jnp.where(live_t, lse_ref[...] * LOG2E, 1e30)
    lanes = lax.broadcasted_iota(jnp.int32, (tokens, HD), 1)
    deltas = jnp.zeros((tokens, HD), jnp.float32)
    for h in range(H):
        at = slice(h * HD, (h + 1) * HD)
        product = do_ref[:, at].astype(jnp.float32) * out_ref[:, at].astype(jnp.float32)
        deltas = jnp.where(lanes == h, jnp.sum(product, 1, keepdims=True), deltas)
    stats[1] = deltas.T[:H]
    swaps[2].start()

    def own_step(i, _):
        j = lax.rem(half * heads + i, KVH)
        head = pl.ds(pl.multiple_of(j * HD, HD), HD)
        stat = pl.ds(pl.multiple_of(j * G, G), G)
        lse_row = rows_to_lanes(stats[0, stat, :])
        delta_row = rows_to_lanes(stats[1, stat, :])

        def keep(chunk, score_low):
            own_low[j, :, chunk] = score_low

        dk, dv = part_grads(
            k_ref[:, head], v_ref[:, head], head_pair(q_ref, j), head_pair(do_ref, j),
            lse_row, delta_row, jnp.concatenate([causal] * 2, 1), keep,
        )
        dk_ref[0, :, head] = dk.astype(jnp.bfloat16)
        dv_ref[0, :, head] = dv.astype(jnp.bfloat16)
        return 0

    lax.fori_loop(0, KVH - 1, own_step, 0)

    def end_gather(d, _):
        gather_copy(d).wait()
        return 0

    lax.fori_loop(1, n, end_gather, 0)
    for copy in swaps:
        copy.wait()

    block = UB if prompt_rows % UB == 0 else prompt_rows

    def part_copy(i, d):
        return pltpu.make_async_remote_copy(
            src_ref=parts.at[i, d],
            dst_ref=landed.at[i, d],
            send_sem=part_send.at[i, d],
            recv_sem=part_recv.at[i, d],
            device_id={"prefix": lax.rem(me + n - d, n)},
            device_id_type=MESH,
        )

    def part_step(i):
        head = slice(i * HD, (i + 1) * HD)
        j = half * heads + i
        own_stat = pl.ds(pl.multiple_of(j * G, G), G)
        other_stat = slice(i * G, (i + 1) * G)
        sides = (
            (head_pair(q_ref, j), head_pair(do_ref, j), stats[0, own_stat], stats[1, own_stat]),
            (
                head_pair(q_other, i), head_pair(do_other, i),
                stats_other[0, other_stat], stats_other[1, other_stat],
            ),
        )

        def block_step(b, _):
            at = pl.ds(pl.multiple_of(b * block, block), block)
            slots = pl.ds(b * (block // rows), block // rows)
            keys = gathered[slots, 0, :, head].reshape(block, HD)
            values = gathered[slots, 1, :, head].reshape(block, HD)
            both = None
            for side, (queries, grads, lse, delta) in enumerate(sides):

                def keep(chunk, score_low):
                    prompt_low[side, i, at, chunk] = score_low

                dk, dv = part_grads(
                    keys, values, queries, grads, rows_to_lanes(lse), rows_to_lanes(delta), None,
                    keep,
                )
                term = jnp.concatenate([dk, dv], 1)
                both = term if both is None else both + term
            parts[i, slots] = both.astype(jnp.bfloat16).reshape(block // rows, rows, 2 * HD)
            return 0

        if prompt_rows == block:
            block_step(0, 0)
        else:
            lax.fori_loop(0, prompt_rows // block, block_step, 0)

        def start_part(d, _):
            part_copy(i, d).start()
            return 0

        lax.fori_loop(1, n, start_part, 0)

    for i in range(heads):
        part_step(i)

    def back_copy(i):
        return pltpu.make_async_remote_copy(
            src_ref=dq_other.at[0, i],
            dst_ref=dq_other.at[1, i],
            send_sem=back_send.at[i],
            recv_sem=back_recv.at[i],
            device_id=partner,
            device_id_type=MESH,
        )

    def prompt_term(side, i):
        keys = gathered[:, 0, :, i * HD : (i + 1) * HD].reshape(prompt_rows, HD)
        return dot(keys.T, prompt_low[side, i])

    def store_queries(j, prompt_sum):
        keys = k_ref[:, pl.ds(pl.multiple_of(j * HD, HD), HD)]
        dq_t = ((prompt_sum + dot(keys.T, own_low[j])) * SCALE).astype(jnp.bfloat16)
        for g in range(G):
            at = pl.ds(pl.multiple_of((j * G + g) * HD, HD), HD)
            dq_ref[0, :, at] = dq_t[:, g * HD : (g + 1) * HD].T

    for i in range(heads):
        dq_other[0, i] = prompt_term(1, i)
        back_copy(i).start()
    own_step(KVH - 1, 0)
    for i in range(heads):
        store_queries(half * heads + i, prompt_term(0, i))
    def sum_step(i, _):
        def wait_part(d, _):
            part_copy(i, d).wait()
            return 0

        lax.fori_loop(1, n, wait_part, 0)
        others = jnp.sum(landed[i, 1:].astype(jnp.float32), 0)
        totals[mine, i] = others + parts[i, 0].astype(jnp.float32)
        return 0

    lax.fori_loop(0, heads, sum_step, 0)

    def total_copy(d):
        return pltpu.make_async_remote_copy(
            src_ref=totals.at[mine],
            dst_ref=totals.at[mine],
            send_sem=total_send.at[d],
            recv_sem=total_recv.at[d],
            device_id={"sample": lax.rem(mine + d, ns)},
            device_id_type=MESH,
        )

    for d in range(1, ns):
        total_copy(d).start()
    for i in range(heads):
        back_copy(i).wait()
        store_queries((1 - half) * heads + i, dq_other[1, i])
    for d in range(1, ns):
        total_copy(d).wait()
    for j in range(KVH):
        both = totals[j // heads, j % heads]
        for s in range(2 + j // heads, ns, 2):
            both = both + totals[s, j % heads]
        pdk_ref[:, j * HD : (j + 1) * HD] = both[:, :HD]
        pdv_ref[:, j * HD : (j + 1) * HD] = both[:, HD:]


def store_kernel(*refs):
    *arrays, sem = refs
    count = len(arrays) // 2
    copies = [
        pltpu.make_async_copy(arrays[i], arrays[count + i], sem.at[i]) for i in range(count)
    ]
    for copy in copies:
        copy.start()
    for copy in copies:
        copy.wait()


def body(resp_q, resp_k, resp_v, resp_do, resp_out, resp_lse, prompt_k, prompt_v, resp_lengths):
    n = lax.axis_size("prefix")
    ns = lax.axis_size("sample")
    rows, width = prompt_k.shape
    _, tokens, q_width = resp_q.shape
    bf16, f32 = jnp.bfloat16, jnp.float32
    heads = KVH // 2
    vmem = pl.BlockSpec(memory_space=pltpu.VMEM)
    hbm = pl.BlockSpec(memory_space=pltpu.HBM)
    dma = pltpu.SemaphoreType.DMA
    out_shape = (
        jax.ShapeDtypeStruct(resp_q.shape, bf16),
        jax.ShapeDtypeStruct(resp_k.shape, bf16),
        jax.ShapeDtypeStruct(resp_v.shape, bf16),
        jax.ShapeDtypeStruct((rows, width), f32),
        jax.ShapeDtypeStruct((rows, width), f32),
    )
    args = (
        resp_lengths, resp_q, resp_k, resp_v, resp_do, resp_out, jnp.swapaxes(resp_lse, 1, 2),
        prompt_k, prompt_v,
    )
    args = args[:1] + tuple(pltpu.with_memory_space_constraint(arg, pltpu.HBM) for arg in args[1:])
    results = pl.pallas_call(
        functools.partial(kernel, n, ns, rows),
        out_shape=tuple(pltpu.VMEM(o.shape, o.dtype) for o in out_shape),
        in_specs=[hbm] * 9,
        out_specs=(vmem,) * 5,
        scratch_shapes=[
            pltpu.SMEM((1,), jnp.int32),
            pltpu.VMEM((tokens, q_width), bf16),
            pltpu.VMEM((tokens, width), bf16),
            pltpu.VMEM((tokens, width), bf16),
            pltpu.VMEM((tokens, q_width), bf16),
            pltpu.VMEM((tokens, q_width), bf16),
            pltpu.VMEM((H, tokens), f32),
            pltpu.VMEM((2, H, tokens), f32),
            pltpu.VMEM((KVH, tokens, G * tokens), bf16),
            pltpu.VMEM((2, heads, n * rows, G * tokens), bf16),
            pltpu.VMEM((tokens, q_width // 2), bf16),
            pltpu.VMEM((tokens, q_width // 2), bf16),
            pltpu.VMEM((2, H // 2, tokens), f32),
            pltpu.VMEM((2, heads, HD, G * tokens), f32),
            pltpu.VMEM((n, 2, rows, heads * HD), bf16),
            pltpu.VMEM((heads, n, rows, 2 * HD), bf16),
            pltpu.VMEM((heads, n, rows, 2 * HD), bf16),
            pltpu.VMEM((ns, heads, rows, 2 * HD), f32),
            dma((9,)),
            dma((n,)),
            dma((n,)),
            dma((3,)),
            dma((3,)),
            dma((heads,)),
            dma((heads,)),
            dma((heads, n)),
            dma((heads, n)),
            dma((ns,)),
            dma((ns,)),
        ],
        compiler_params=pltpu.CompilerParams(
            collective_id=0, has_side_effects=True, vmem_limit_bytes=48 * 1024 * 1024
        ),
        cost_estimate=pl.CostEstimate(
            flops=2_000_000_000, bytes_accessed=5_000_000, transcendentals=1_600_000
        ),
    )(*args)
    return pl.pallas_call(
        store_kernel,
        out_shape=out_shape,
        in_specs=[vmem] * 5,
        out_specs=(hbm,) * 5,
        scratch_shapes=[dma((5,))],
        compiler_params=pltpu.CompilerParams(vmem_limit_bytes=4 * 1024 * 1024),
    )(*(pltpu.with_memory_space_constraint(array, pltpu.VMEM) for array in results))


def solution(mesh):
    rows = P(("sample", "prefix"), None, None)
    prompt = P("prefix", None)
    return jax.shard_map(
        body,
        mesh=mesh,
        in_specs=(rows, rows, rows, rows, rows, rows, prompt, prompt, P(("sample", "prefix"))),
        out_specs=(rows, rows, rows, prompt, prompt),
        check_vma=False,
    )
```
